128 devices in a mesh: row: 16 (over z_lo, y, core), col: 8 (over z_hi, x).
Axes of the slice: x: 4, y: 4, z: 4 (z_hi: 2, z_lo: 2; z = z_hi * 2 + z_lo), core: 2. Of those that a mesh axis runs over, the one named last changes fastest.
Arguments:
- a_tiles: bfloat16 [2048, 32, 64, 64], P('row', 'col'), may hold values from -6 to 6
- a_cols: int32 [2048, 32], P('row', 'col'), may hold values from 0 to 2047, as said below
- p_tiles: bfloat16 [2048, 64, 64], P(('col', 'row')), may hold values from -0.75 to 0.75
- agg_sizes: int32 [16, 16], P('row'), may hold values from 1 to 24, 128 in all within a row
Outputs:
- coarse: float32 [256, 64, 16384], P(None, None, ('col', 'row'))
The draws below stay inside these ranges and needn't reach their ends.
Inputs may be any that keep to these rules, and one draw needn't show every extreme that they name: a_cols[i, s] is a fine block of column group s // 4: from (s // 4) * 256 to (s // 4 + 1) * 256 - 1.
All inputs are finite; a program needn't handle non-finite values.
Results may differ from the reference program's by a relative error of at most 0.0029.
Values may be sent and summed in bfloat16 or wider, within the bound.
A program may use at most 192 MiB of HBM per device.

```python
import math
import jax
import jax.numpy as jnp
import numpy as np
from jax import lax

B = 64
FR = 128
KC = 4
CR = 16
MOSTAGG = 24
NF = 2048
FC = 256
SLOTS = 32
NC = 256
N_ROW = 16


def draw_a_cols(key, part):
    key = jax.random.fold_in(key, 11)
    spread = jax.random.randint(key, (NF, SLOTS), 0, FC // 2, dtype=jnp.int32)
    rows_here = jnp.arange(NF, dtype=jnp.int32) % FR
    centre = rows_here * (FC // FR) - FC // 4
    offsets = (centre[:, None] + spread) % FC
    owner = jnp.arange(SLOTS, dtype=jnp.int32) // KC
    return (owner[None, :] * FC + offsets).astype(jnp.int32)


def level_of(rng, extent, cuts, least, largest):
    factor_of = 1.0
    for dim, parts in cuts:
        heights = jax.random.uniform(jax.random.fold_in(jax.random.fold_in(rng, 6), dim), (parts,), jnp.float32, least / len(cuts), largest / len(cuts))
        factor_of = factor_of * jnp.repeat(jnp.exp(heights), extent[dim] // parts).reshape((-1,) + (1,) * (len(extent) - 1 - dim))
    return factor_of


def profile(amount, total, bound, slope):
    weights = [(1 << 20) // math.isqrt(rank ** slope) + 1 for rank in range(2, amount + 1)]
    spare, given = total - bound - (amount - 1), [1] * (amount - 1)
    while spare > 0:
        free = [i for i in range(amount - 1) if given[i] < bound]
        mass, remaining = sum([weights[i] for i in free]), spare
        for i in free:
            addition = min(bound - given[i], max(1, remaining * weights[i] // mass), spare)
            given[i] = given[i] + addition
            spare = spare - addition
    return np.array([bound] + given)


def ragged(rng, count, total, most, skew):
    if count == 2:
        one = jax.random.randint(rng, (), max(1, total - most), min(most, total - 1) + 1)
        return jnp.stack([one, total - one])
    sizes = jnp.asarray(profile(count, total, most, skew), jnp.int32)
    twos = (count - 1) // 2
    donor, sink = sizes[1:1 + 2 * twos:2], sizes[2:2 + 2 * twos:2]
    slack = jnp.minimum(donor - 1, most - sink)
    shifted = jax.random.randint(jax.random.fold_in(rng, 1), (twos,), 0, 1 << 20) % (slack + 1)
    sizes = sizes.at[1:1 + 2 * twos:2].set(donor - shifted).at[2:2 + 2 * twos:2].set(sink + shifted)
    return sizes[jax.random.permutation(jax.random.fold_in(rng, 2), count)]


def centred(rng, shape, scale, reach, cuts=(), kind=jnp.bfloat16):
    array = jax.random.normal(rng, shape, jnp.float32) * scale
    if len(cuts) > 0:
        array = level_of(rng, shape, cuts, -0.22, 0.18) * array
    return jnp.clip(array, min=-reach, max=reach).astype(kind)


def setup_inputs(seed: int = 0) -> dict:
    keys = jax.random.split(jax.random.key(seed), 5)
    a_tiles = centred(keys[0], (NF, SLOTS, B, B), 1.0, 6.0, ((0, 16), (1, 8)))
    a_cols = draw_a_cols(jax.random.fold_in(keys[4], 71), 0)
    p_tiles = centred(keys[2], (NF, B, B), B ** -0.5, 0.75, ((0, 128),))
    agg_sizes = jax.vmap(lambda own: ragged(own, CR, FR, MOSTAGG, 2))(jax.random.split(keys[3], N_ROW)).reshape((N_ROW, CR)).astype(jnp.int32)
    return {"a_tiles": a_tiles, "a_cols": a_cols, "p_tiles": p_tiles, "agg_sizes": agg_sizes}


def reference(a_tiles, a_cols, p_tiles, agg_sizes):
    ends = jnp.cumsum(agg_sizes, axis=1)
    places = jnp.arange(FR, dtype=jnp.int32)
    local = jnp.sum((ends[:, None, :] <= places[None, :, None]).astype(jnp.int32), axis=2)
    coarse_of = (local + jnp.arange(N_ROW, dtype=jnp.int32)[:, None] * CR).reshape(NF).astype(jnp.int32)

    def group(index):
        start = (index * FR).astype(jnp.int32)
        tiles = lax.dynamic_slice_in_dim(a_tiles, start, FR, 0).reshape(FR * SLOTS, B, B).astype(jnp.float32)
        columns = lax.dynamic_slice_in_dim(a_cols, start, FR, 0).reshape(FR * SLOTS).astype(jnp.int32)
        right = jnp.take(p_tiles, columns, axis=0).astype(jnp.float32)
        left = lax.dynamic_slice_in_dim(p_tiles, start, FR, 0).astype(jnp.float32)
        product = jnp.einsum("sij,sjk->sik", tiles, right, precision=lax.Precision.HIGHEST)
        product = lax.optimization_barrier(product.astype(jnp.bfloat16)).astype(jnp.float32)
        product = product.reshape(FR, SLOTS, B, B)
        pieces = jnp.einsum("fuv,fkuw->fkvw", left, product, precision=lax.Precision.HIGHEST)
        pieces = pieces.reshape(FR * SLOTS, B, B)
        row_local = lax.dynamic_slice_in_dim(coarse_of, start, FR, 0) - index * CR
        row_local = jnp.repeat(row_local, SLOTS)
        target = (row_local * NC + jnp.take(coarse_of, columns, axis=0)).astype(jnp.int32)
        summed = jax.ops.segment_sum(pieces, target, num_segments=CR * NC)
        return summed.reshape(CR, NC, B, B).transpose(0, 2, 1, 3).reshape(CR, B, NC * B)

    blocks = lax.map(group, jnp.arange(N_ROW, dtype=jnp.int32))
    return blocks.reshape(NC, B, NC * B)
```

```python
import functools

import jax
import jax.numpy as jnp
from jax import lax
from jax.experimental import pallas as pl
from jax.experimental.pallas import tpu as pltpu
from jax.sharding import PartitionSpec as P

MESH = pl.DeviceIdType.MESH
ROWS = 16
COLS = 8
MIB = 1 << 20


def spread_kernel(p_ref, s_ref, col_out, row_out, mine, send_sem, col_sem, row_sem, local_sem):
    row = lax.axis_index("row")
    col = lax.axis_index("col")
    owner = (2 * col + row // 8) % ROWS
    barrier = pltpu.get_barrier_semaphore()

    @pl.loop(1, ROWS)
    def _(step):
        pl.semaphore_signal(barrier, 1, device_id=((row + step) % ROWS, col), device_id_type=MESH)

    @pl.loop(0, 8)
    def _(step):
        src = (8 * (row % 2) + step, row // 2)

        @pl.when(jnp.logical_or(src[0] != row, src[1] != col))
        def _():
            pl.semaphore_signal(barrier, 1, device_id=src, device_id_type=MESH)

    for k in range(8):
        mine[pl.ds(64 * k, 64), :] = jnp.concatenate([p_ref[2 * k], p_ref[2 * k + 1]], axis=-1)
    mine[pl.ds(512, 16), :] = s_ref[...]
    self_send = jnp.logical_and(row == owner, True)
    pl.semaphore_wait(barrier, ROWS - 1 + 8 - jnp.where(self_send, 1, 0))

    own = pltpu.make_async_copy(mine, col_out.at[row], local_sem.at[0])
    own.start()

    def col_copy(step):
        return pltpu.make_async_remote_copy(
            src_ref=mine,
            dst_ref=col_out.at[row],
            send_sem=send_sem.at[step],
            recv_sem=col_sem.at[row],
            device_id=((row + step) % ROWS, col),
            device_id_type=MESH,
        )

    def row_copy(step):
        return pltpu.make_async_remote_copy(
            src_ref=mine.at[pl.ds(0, 512)],
            dst_ref=row_out.at[row % 8],
            send_sem=send_sem.at[ROWS + step],
            recv_sem=row_sem.at[row % 8],
            device_id=(owner, (col + step) % COLS),
            device_id_type=MESH,
        )

    def row_local():
        return pltpu.make_async_copy(mine.at[pl.ds(0, 512)], row_out.at[row % 8], local_sem.at[1])

    @pl.loop(1, ROWS)
    def _(step):
        col_copy(step).start()

    @pl.when(self_send)
    def _():
        row_local().start()

    @pl.when(jnp.logical_not(self_send))
    def _():
        row_copy(0).start()

    @pl.loop(1, COLS)
    def _(step):
        row_copy(step).start()

    own.wait()

    @pl.when(self_send)
    def _():
        row_local().wait()

    @pl.when(jnp.logical_not(self_send))
    def _():
        row_copy(0).wait_send()

    @pl.loop(1, COLS)
    def _(step):
        row_copy(step).wait_send()

    @pl.loop(1, ROWS)
    def _(step):
        col_copy(step).wait_send()
        src = (row + step) % ROWS
        pltpu.make_async_copy(col_out.at[src], col_out.at[src], col_sem.at[src]).wait()

    @pl.loop(0, 8)
    def _(step):
        src = (8 * (row % 2) + step, row // 2)

        @pl.when(jnp.logical_or(src[0] != row, src[1] != col))
        def _():
            pltpu.make_async_copy(row_out.at[step], row_out.at[step], row_sem.at[step]).wait()


def spread(p_tiles, sizes):
    return pl.pallas_call(
        spread_kernel,
        out_shape=(
            jax.ShapeDtypeStruct((ROWS, 528, 128), jnp.bfloat16),
            jax.ShapeDtypeStruct((8, 512, 128), jnp.bfloat16),
        ),
        in_specs=[pl.BlockSpec(memory_space=pltpu.VMEM)] * 2,
        out_specs=[pl.BlockSpec(memory_space=pl.ANY)] * 2,
        scratch_shapes=[
            pltpu.VMEM((528, 128), jnp.bfloat16),
            pltpu.SemaphoreType.DMA((ROWS + COLS,)),
            pltpu.SemaphoreType.DMA((ROWS,)),
            pltpu.SemaphoreType.DMA((8,)),
            pltpu.SemaphoreType.DMA((2,)),
        ],
        compiler_params=pltpu.CompilerParams(collective_id=0, has_side_effects=True),
    )(p_tiles, sizes)


CHUNK = 16


def blocks_kernel(cols_ref, mine_ref, sizes_ref, a_hbm, col_ref, row_ref, out_hbm,
                  a_buf, table, left, acc, out_buf, bmap, amap, a_sem, out_sem):
    chunks = 128 // CHUNK

    def a_copy(k):
        return pltpu.make_async_copy(
            a_hbm.at[pl.ds(CHUNK * k, CHUNK)], a_buf.at[pl.ds(CHUNK * k, CHUNK)], a_sem.at[k]
        )

    for k in range(chunks):
        a_copy(k).start()

    @pl.loop(0, 256, unroll=8)
    def _(k):
        acc[pl.ds(64 * k, 64), :] = jnp.zeros((64, 128), jnp.float32)

    def walk(total, size_of, put):
        def step(f, state):
            at, end = state
            go = f >= end
            at = jnp.where(go, at + 1, at)
            end = jnp.where(go, end + size_of(jnp.minimum(at, 31)), end)
            put(f, at)
            return at, end

        lax.fori_loop(0, total, step, (jnp.int32(0), size_of(0)))

    def put_b(f, at):
        bmap[f] = at

    def put_a(f, at):
        amap[f] = at

    walk(256, lambda k: sizes_ref[k // 16, k % 16], put_b)
    walk(128, lambda k: mine_ref[0, k % 16], put_a)

    lane = lax.broadcasted_iota(jnp.int32, (64, 128), 1)
    zero = jnp.zeros((64, 128), jnp.bfloat16)

    @pl.loop(0, 128, unroll=2)
    def _(k):
        pair = col_ref[k // 8, pl.ds(pl.multiple_of(64 * (k % 8), 64), 64), :]
        turned = jnp.concatenate([pair[:, 64:], pair[:, :64]], axis=-1)
        right0 = bmap[2 * k] % 2
        right1 = bmap[2 * k + 1] % 2
        keep0 = (lane // 64) == right0
        keep1 = (lane // 64) == right1
        first = jnp.where(right0 == 0, pair, turned)
        second = jnp.where(right1 == 0, turned, pair)
        table[2 * k] = jnp.where(keep0, first, zero)
        table[2 * k + 1] = jnp.where(keep1, second, zero)
        own = row_ref[k // 16, pl.ds(pl.multiple_of(64 * (k % 8), 64), 64), :] if False else None

    @pl.loop(0, 64, unroll=2)
    def _(k):
        own = row_ref[k // 8, pl.ds(pl.multiple_of(64 * (k % 8), 64), 64), :]
        left[k] = own.T

    base = lax.axis_index("col") * 256
    group = 4

    @pl.loop(0, chunks)
    def _(chunk):
        a_copy(chunk).wait()

        @pl.loop(0, CHUNK // group)
        def _(step):
            first = chunk * CHUNK + step * group
            products = []
            for r in range(group):
                row = []
                for s in range(4):
                    j = cols_ref[first + r, s] - base
                    row.append(
                        jnp.dot(
                            a_buf[first + r, s], table[j], preferred_element_type=jnp.float32
                        ).astype(jnp.bfloat16)
                    )
                products.append(row)
            pieces = []
            for r in range(group):
                i = first + r
                pt = left[i // 2, pl.ds(pl.multiple_of(64 * (r % 2), 64), 64), :]
                pieces.append(
                    jnp.dot(pt, jnp.concatenate(products[r], axis=-1), preferred_element_type=jnp.float32)
                )
            for r in range(group):
                i = first + r
                a = amap[i]
                for s in range(4):
                    b = bmap[cols_ref[i, s] - base]
                    at = pl.multiple_of(((b // 2) * 16 + a) * 64, 64)
                    acc[pl.ds(at, 64), :] += pieces[r][:, 128 * s:128 * s + 128]

    for d in range(ROWS):
        out_buf[d] = acc[pl.ds(1024 * d, 1024), :].astype(jnp.bfloat16)
        pltpu.make_async_copy(out_buf.at[d], out_hbm.at[d], out_sem.at[d]).start()
    for d in range(ROWS):
        pltpu.make_async_copy(out_buf.at[d], out_hbm.at[d], out_sem.at[d]).wait()


def blocks(a_cols, mine, sizes, a_tiles, col_p, row_p):
    smem = pl.BlockSpec(memory_space=pltpu.SMEM)
    vmem = pl.BlockSpec(memory_space=pltpu.VMEM)
    hbm = pl.BlockSpec(memory_space=pl.ANY)
    return pl.pallas_call(
        blocks_kernel,
        out_shape=jax.ShapeDtypeStruct((ROWS, 1024, 128), jnp.bfloat16),
        in_specs=[smem, smem, smem, hbm, vmem, vmem],
        out_specs=hbm,
        scratch_shapes=[
            pltpu.VMEM((128, 4, 64, 64), jnp.bfloat16),
            pltpu.VMEM((256, 64, 128), jnp.bfloat16),
            pltpu.VMEM((64, 128, 64), jnp.bfloat16),
            pltpu.VMEM((ROWS * 1024, 128), jnp.float32),
            pltpu.VMEM((ROWS, 1024, 128), jnp.bfloat16),
            pltpu.SMEM((256,), jnp.int32),
            pltpu.SMEM((128,), jnp.int32),
            pltpu.SemaphoreType.DMA((128 // CHUNK,)),
            pltpu.SemaphoreType.DMA((ROWS,)),
        ],
        compiler_params=pltpu.CompilerParams(vmem_limit_bytes=56 * MIB),
    )(a_cols, mine, sizes, a_tiles, col_p, row_p)


def exchange_kernel(src_ref, out_ref, send_sem, recv_sem, local_sem):
    row = lax.axis_index("row")
    col = lax.axis_index("col")
    barrier = pltpu.get_barrier_semaphore()

    @pl.loop(1, ROWS)
    def _(step):
        pl.semaphore_signal(barrier, 1, device_id=((row + step) % ROWS, col), device_id_type=MESH)

    pl.semaphore_wait(barrier, ROWS - 1)
    own = pltpu.make_async_copy(src_ref.at[row], out_ref.at[row], local_sem)
    own.start()

    def copy(step):
        to = (row + step) % ROWS
        return pltpu.make_async_remote_copy(
            src_ref=src_ref.at[to],
            dst_ref=out_ref.at[row],
            send_sem=send_sem.at[step],
            recv_sem=recv_sem.at[row],
            device_id=(to, col),
            device_id_type=MESH,
        )

    @pl.loop(1, ROWS)
    def _(step):
        copy(step).start()

    own.wait()

    @pl.loop(1, ROWS)
    def _(step):
        copy(step).wait_send()
        src = (row + step) % ROWS
        pltpu.make_async_copy(out_ref.at[src], out_ref.at[src], recv_sem.at[src]).wait()


def exchange(parts):
    return pl.pallas_call(
        exchange_kernel,
        out_shape=jax.ShapeDtypeStruct(parts.shape, parts.dtype),
        in_specs=[pl.BlockSpec(memory_space=pl.ANY)],
        out_specs=pl.BlockSpec(memory_space=pl.ANY),
        scratch_shapes=[
            pltpu.SemaphoreType.DMA((ROWS,)),
            pltpu.SemaphoreType.DMA((ROWS,)),
            pltpu.SemaphoreType.DMA,
        ],
        compiler_params=pltpu.CompilerParams(collective_id=1, has_side_effects=True),
    )(parts)


def per_device(a_tiles, a_cols, p_tiles, agg_sizes):
    col = lax.axis_index("col")
    sizes = jnp.zeros((16, 128), jnp.bfloat16).at[0, :16].set(agg_sizes[0].astype(jnp.bfloat16))
    col_p, row_p = spread(p_tiles, sizes)
    col_sizes = lax.dynamic_slice(col_p, (2 * col, 512, 0), (2, 1, 16))[:, 0, :].astype(jnp.int32)
    parts = blocks(a_cols, agg_sizes, col_sizes, a_tiles, col_p, row_p)
    got = exchange(parts)
    return got.reshape(256, 64, 128).astype(jnp.float32)


def solution(mesh):
    return jax.shard_map(
        per_device,
        mesh=mesh,
        in_specs=(
            P("row", "col", None, None),
            P("row", "col"),
            P(("col", "row"), None, None),
            P("row", None),
        ),
        out_specs=P(None, None, ("col", "row")),
        check_vma=False,
    )
```

```python
import jax
import jax.numpy as jnp
from jax import lax
from jax.experimental import pallas as pl
from jax.experimental.pallas import tpu as pltpu
from jax.sharding import PartitionSpec as P

MESH = pl.DeviceIdType.MESH
ROWS = 16
COLS = 8
MIB = 1 << 20
PITCH = 136
BF = jnp.bfloat16
F32 = jnp.float32


def place(zl, y, core, zh, x):
    return (zl * 8 + y * 2 + core, zh * 4 + x)


def spread_kernel(p_ref, s_ref, a_hbm, col_out, row_out, a_out,
                  mine, pad, a_in, mid, a_buf,
                  send_sem, col_sem, row_sem, local_sem, a_sem, out_sem):
    row = lax.axis_index("row")
    col = lax.axis_index("col")
    zl, y, core = row // 8, (row // 2) % 4, row % 2
    zh, x = col // 4, col % 4

    sibling = place(zl, y, 1 - core, zh, x)
    partner = place(1 - zl, y, core, zh, x)
    along_y = [place(zl, (y + d) % 4, core, zh, x) for d in (1, 3, 2)]
    across = place(zl, y, core, 1 - zh, x)
    along_x = [place(zl, y, core, zh, (x + d) % 4) for d in (1, 3, 2)]
    to = place(zh, x, zl, core, y)
    source = place(core, x, zh, zl, y)
    stays = jnp.logical_and(to[0] == row, to[1] == col)
    moves = jnp.logical_not(stays)

    for k in range(8):
        a_copy = pltpu.make_async_copy(
            a_hbm.at[:, pl.ds(8 * k, 8)], a_in.at[:, pl.ds(8 * k, 8)], a_sem.at[k]
        )
        a_copy.start()

    barrier = pltpu.get_barrier_semaphore()
    for there in [sibling, partner, *along_y, across, *along_x]:
        pl.semaphore_signal(barrier, 1, device_id=there, device_id_type=MESH)

    @pl.when(moves)
    def _():
        pl.semaphore_signal(barrier, 1, device_id=source, device_id_type=MESH)

    for k in range(8):
        mine[pl.ds(64 * k, 64), :] = jnp.concatenate([p_ref[2 * k], p_ref[2 * k + 1]], axis=-1)
    pad[...] = jnp.zeros_like(pad)
    pad[0:1, 0:16] = s_ref[...].astype(F32)
    mine[pl.ds(512, 16), :] = pad[...].astype(BF)

    pl.semaphore_wait(barrier, 9 + jnp.where(stays, 0, 1))

    count = [0]
    sent = []

    def send(src, dst, sem, there):
        k = count[0]
        count[0] += 1
        copy = pltpu.make_async_remote_copy(
            src_ref=src, dst_ref=dst, send_sem=send_sem.at[k], recv_sem=sem,
            device_id=there, device_id_type=MESH,
        )
        copy.start()
        sent.append(copy)

    def col_slot(index):
        return col_out.at[index]

    def arrived(ref, sem):
        pltpu.make_async_copy(ref, ref, sem).wait()

    def row_of(a, b, c):
        return a * 8 + b * 2 + c

    held = 2 * x + zh
    first = pltpu.make_async_remote_copy(
        src_ref=mine.at[pl.ds(0, 512)], dst_ref=row_out.at[2 * y + core],
        send_sem=send_sem.at[24], recv_sem=row_sem.at[2 * y + core],
        device_id=to, device_id_type=MESH,
    )
    first_here = pltpu.make_async_copy(
        mine.at[pl.ds(0, 512)], row_out.at[2 * y + core], row_sem.at[2 * y + core]
    )

    @pl.when(moves)
    def _():
        first.start()

    @pl.when(stays)
    def _():
        first_here.start()

    for there in [partner, *along_y, sibling]:
        send(mine, col_slot(row), col_sem.at[row], there)
    own = pltpu.make_async_copy(mine, col_slot(row), local_sem)
    own.start()

    eye = (
        lax.broadcasted_iota(jnp.int32, (128, 128), 0)
        == lax.broadcasted_iota(jnp.int32, (128, 128), 1)
    ).astype(BF)

    def turn(k):
        pltpu.make_async_copy(
            a_hbm.at[:, pl.ds(8 * k, 8)], a_in.at[:, pl.ds(8 * k, 8)], a_sem.at[k]
        ).wait()

        @pl.loop(0, 8)
        def _(n):
            u = 8 * k + n
            wide = jnp.concatenate([a_in[s, u] for s in range(4)], axis=0)
            tiles = lax.dot_general(eye, wide, (((1,), (1,)), ((), ())), preferred_element_type=F32)
            for h in range(2):
                mid[h, pl.ds(pl.multiple_of(PITCH * u, 8), 128), :] = tiles[:, 128 * h:128 * h + 128]

    def pick(k):
        @pl.loop(0, 32)
        def _(n):
            i = 32 * k + n
            for h in range(2):
                a_buf[i, :, 128 * h:128 * h + 128] = mid[h, pl.ds(i, 64, stride=PITCH), :].astype(BF)

        pltpu.make_async_copy(
            a_buf.at[pl.ds(32 * k, 32)], a_out.at[pl.ds(32 * k, 32)], out_sem.at[k]
        ).start()

    turn(0)
    turn(1)

    other = row_of(1 - zl, y, core)
    arrived(col_slot(other), col_sem.at[other])
    for there in [*along_y, sibling]:
        send(col_slot(other), col_slot(other), col_sem.at[other], there)
    arrived(row_out.at[held], row_sem.at[held])
    for there in [across, *along_x]:
        send(row_out.at[held], row_out.at[held], row_sem.at[held], there)

    turn(2)
    turn(3)

    across_held = 2 * x + 1 - zh
    arrived(row_out.at[across_held], row_sem.at[across_held])
    for there in along_x:
        send(row_out.at[across_held], row_out.at[across_held], row_sem.at[across_held], there)

    turn(4)
    turn(5)
    for d in (1, 3, 2):
        index = row_of(zl, (y + d) % 4, core)
        arrived(col_slot(index), col_sem.at[index])
        send(col_slot(index), col_slot(index), col_sem.at[index], sibling)
    turn(6)
    turn(7)
    pick(0)
    pick(1)
    for d in (1, 3, 2):
        index = row_of(1 - zl, (y + d) % 4, core)
        arrived(col_slot(index), col_sem.at[index])
        send(col_slot(index), col_slot(index), col_sem.at[index], sibling)
    pick(2)
    pick(3)

    own.wait()
    for a in (0, 1):
        for b in range(4):
            index = row_of(a, b, 1 - core)
            arrived(col_slot(index), col_sem.at[index])
    for d in (1, 3, 2):
        for h in (0, 1):
            index = 2 * ((x + d) % 4) + h
            arrived(row_out.at[index], row_sem.at[index])

    @pl.when(moves)
    def _():
        first.wait_send()

    for copy in sent:
        copy.wait_send()
    for k in range(4):
        pltpu.make_async_copy(
            a_buf.at[pl.ds(32 * k, 32)], a_out.at[pl.ds(32 * k, 32)], out_sem.at[k]
        ).wait()


def spread(p_tiles, sizes, a_turned):
    vmem = pl.BlockSpec(memory_space=pltpu.VMEM)
    hbm = pl.BlockSpec(memory_space=pl.ANY)
    return pl.pallas_call(
        spread_kernel,
        out_shape=(
            jax.ShapeDtypeStruct((ROWS, 528, 128), BF),
            jax.ShapeDtypeStruct((8, 512, 128), BF),
            jax.ShapeDtypeStruct((128, 64, 256), BF),
        ),
        in_specs=[vmem, vmem, hbm],
        out_specs=[hbm] * 3,
        scratch_shapes=[
            pltpu.VMEM((528, 128), BF),
            pltpu.VMEM((16, 128), F32),
            pltpu.VMEM((4, 64, 64, 128), BF),
            pltpu.VMEM((2, 64 * PITCH, 128), F32),
            pltpu.VMEM((128, 64, 256), BF),
            pltpu.SemaphoreType.DMA((25,)),
            pltpu.SemaphoreType.DMA((ROWS,)),
            pltpu.SemaphoreType.DMA((8,)),
            pltpu.SemaphoreType.DMA,
            pltpu.SemaphoreType.DMA((8,)),
            pltpu.SemaphoreType.DMA((4,)),
        ],
        compiler_params=pltpu.CompilerParams(
            collective_id=0, has_side_effects=True, vmem_limit_bytes=24 * MIB
        ),
    )(p_tiles, sizes, a_turned)


CHUNK = 16


def blocks_kernel(cols_ref, a_hbm, col_ref, row_ref, out_hbm,
                  a_buf, table, left, acc, out_buf, maps, smaps, a_sem, out_sem, map_sem):
    chunks = 128 // CHUNK
    row = lax.axis_index("row")
    col = lax.axis_index("col")

    def a_copy(k):
        return pltpu.make_async_copy(
            a_hbm.at[pl.ds(CHUNK * k, CHUNK)], a_buf.at[pl.ds(CHUNK * k, CHUNK)], a_sem.at[k]
        )

    for k in range(chunks):
        a_copy(k).start()

    lower = (
        lax.broadcasted_iota(jnp.int32, (16, 128), 1) <= lax.broadcasted_iota(jnp.int32, (16, 128), 0)
    )
    fine = lax.broadcasted_iota(jnp.int32, (16, 128), 1).astype(F32)

    def aggregates(index):
        sizes = col_ref[index, pl.ds(512, 16), :].astype(F32)[0:1, :]
        ends = jnp.sum(jnp.where(lower, sizes, 0.0), axis=1, keepdims=True)
        return jnp.sum(jnp.where(ends <= fine, 1.0, 0.0), axis=0, keepdims=True).astype(jnp.int32)

    maps[0:1, :] = aggregates(2 * col)
    maps[1:2, :] = aggregates(2 * col + 1) + 16
    maps[2:3, :] = aggregates(row)
    to_smem = pltpu.make_async_copy(maps, smaps, map_sem)
    to_smem.start()

    @pl.loop(0, 256, unroll=8)
    def _(k):
        acc[pl.ds(64 * k, 64), :] = jnp.zeros((64, 128), F32)

    @pl.loop(0, 64, unroll=2)
    def _(k):
        own = row_ref[k // 8, pl.ds(pl.multiple_of(64 * (k % 8), 64), 64), :]
        left[k] = own.T

    lane = lax.broadcasted_iota(jnp.int32, (64, 128), 1)
    zero = jnp.zeros((64, 128), BF)
    to_smem.wait()

    @pl.loop(0, 128, unroll=2)
    def _(k):
        pair = col_ref[k // 8, pl.ds(pl.multiple_of(64 * (k % 8), 64), 64), :]
        turned = jnp.concatenate([pair[:, 64:], pair[:, :64]], axis=-1)
        right0 = smaps[k // 64, 2 * (k % 64)] % 2
        right1 = smaps[k // 64, 2 * (k % 64) + 1] % 2
        keep0 = (lane // 64) == right0
        keep1 = (lane // 64) == right1
        first = jnp.where(right0 == 0, pair, turned)
        second = jnp.where(right1 == 0, turned, pair)
        table[2 * k] = jnp.where(keep0, first, zero)
        table[2 * k + 1] = jnp.where(keep1, second, zero)

    base = col * 256
    group = 4

    @pl.loop(0, chunks)
    def _(chunk):
        a_copy(chunk).wait()

        @pl.loop(0, CHUNK // group)
        def _(step):
            first = chunk * CHUNK + step * group
            products = []
            for r in range(group):
                for h in range(2):
                    j0 = cols_ref[2 * h, first + r] - base
                    j1 = cols_ref[2 * h + 1, first + r] - base
                    right = jnp.concatenate(
                        [
                            jnp.concatenate([table[j0], zero], axis=1),
                            jnp.concatenate([zero, table[j1]], axis=1),
                        ],
                        axis=0,
                    )
                    products.append(
                        jnp.dot(
                            a_buf[first + r, :, 128 * h:128 * h + 128], right,
                            preferred_element_type=F32,
                        ).astype(BF)
                    )
            pieces = []
            for r in range(group):
                i = first + r
                pt = left[i // 2, pl.ds(pl.multiple_of(64 * (r % 2), 64), 64), :]
                for h in range(2):
                    pieces.append(jnp.dot(pt, products[2 * r + h], preferred_element_type=F32))
            for r in range(group):
                i = first + r
                a = smaps[2, i]
                for s in range(4):
                    j = cols_ref[s, i] - base
                    b = smaps[j // 128, j % 128]
                    at = pl.multiple_of(((b // 2) * 16 + a) * 64, 64)
                    acc[pl.ds(at, 64), :] += pieces[2 * r + s // 2][:, 128 * (s % 2):128 * (s % 2) + 128]

    for d in range(ROWS):
        out_buf[d] = acc[pl.ds(1024 * d, 1024), :].astype(BF)
        pltpu.make_async_copy(out_buf.at[d], out_hbm.at[d], out_sem.at[d]).start()
    for d in range(ROWS):
        pltpu.make_async_copy(out_buf.at[d], out_hbm.at[d], out_sem.at[d]).wait()


def blocks(a_cols, a_rows, col_p, row_p):
    smem = pl.BlockSpec(memory_space=pltpu.SMEM)
    vmem = pl.BlockSpec(memory_space=pltpu.VMEM)
    hbm = pl.BlockSpec(memory_space=pl.ANY)
    return pl.pallas_call(
        blocks_kernel,
        out_shape=jax.ShapeDtypeStruct((ROWS, 1024, 128), BF),
        in_specs=[smem, hbm, vmem, vmem],
        out_specs=hbm,
        scratch_shapes=[
            pltpu.VMEM((128, 64, 256), BF),
            pltpu.VMEM((256, 64, 128), BF),
            pltpu.VMEM((64, 128, 64), BF),
            pltpu.VMEM((ROWS * 1024, 128), F32),
            pltpu.VMEM((ROWS, 1024, 128), BF),
            pltpu.VMEM((8, 128), jnp.int32),
            pltpu.SMEM((8, 128), jnp.int32),
            pltpu.SemaphoreType.DMA((128 // CHUNK,)),
            pltpu.SemaphoreType.DMA((ROWS,)),
            pltpu.SemaphoreType.DMA,
        ],
        compiler_params=pltpu.CompilerParams(vmem_limit_bytes=32 * MIB),
    )(a_cols, a_rows, col_p, row_p)


def exchange_kernel(src_ref, out_ref, send_sem, recv_sem, local_sem):
    row = lax.axis_index("row")
    col = lax.axis_index("col")
    barrier = pltpu.get_barrier_semaphore()

    @pl.loop(1, ROWS)
    def _(step):
        pl.semaphore_signal(barrier, 1, device_id=((row + step) % ROWS, col), device_id_type=MESH)

    pl.semaphore_wait(barrier, ROWS - 1)
    own = pltpu.make_async_copy(src_ref.at[row], out_ref.at[row], local_sem)
    own.start()

    def copy(step):
        to = (row + step) % ROWS
        return pltpu.make_async_remote_copy(
            src_ref=src_ref.at[to],
            dst_ref=out_ref.at[row],
            send_sem=send_sem.at[step],
            recv_sem=recv_sem.at[row],
            device_id=(to, col),
            device_id_type=MESH,
        )

    @pl.loop(1, ROWS)
    def _(step):
        copy(step).start()

    own.wait()

    @pl.loop(1, ROWS)
    def _(step):
        copy(step).wait_send()
        src = (row + step) % ROWS
        pltpu.make_async_copy(out_ref.at[src], out_ref.at[src], recv_sem.at[src]).wait()


def exchange(parts):
    return pl.pallas_call(
        exchange_kernel,
        out_shape=jax.ShapeDtypeStruct(parts.shape, parts.dtype),
        in_specs=[pl.BlockSpec(memory_space=pl.ANY)],
        out_specs=pl.BlockSpec(memory_space=pl.ANY),
        scratch_shapes=[
            pltpu.SemaphoreType.DMA((ROWS,)),
            pltpu.SemaphoreType.DMA((ROWS,)),
            pltpu.SemaphoreType.DMA,
        ],
        compiler_params=pltpu.CompilerParams(
            collective_id=1, has_side_effects=True, vmem_limit_bytes=MIB
        ),
    )(parts)


def per_device(a_tiles, a_cols, p_tiles, agg_sizes):
    col_p, row_p, a_rows = spread(p_tiles, agg_sizes, a_tiles.transpose(1, 2, 3, 0))
    parts = blocks(a_cols.T, a_rows, col_p, row_p)
    got = exchange(parts)
    return got.reshape(256, 64, 128).astype(F32)


def solution(mesh):
    return jax.shard_map(
        per_device,
        mesh=mesh,
        in_specs=(
            P("row", "col", None, None),
            P("row", "col"),
            P(("col", "row"), None, None),
            P("row", None),
        ),
        out_specs=P(None, None, ("col", "row")),
        check_vma=False,
    )
```

```python
import jax
import jax.numpy as jnp
from jax import lax
from jax.experimental import pallas as pl
from jax.experimental.pallas import tpu as pltpu
from jax.sharding import PartitionSpec as P

MESH = pl.DeviceIdType.MESH
ROWS = 16
COLS = 8
MIB = 1 << 20
PITCH = 136
TILES = 512
GROUP = 8
BF = jnp.bfloat16
F32 = jnp.float32
I32 = jnp.int32

ORDER = [
    (0, 1, 0), (0, 3, 0), (1, 0, 0), (1, 2, 0), (0, 2, 0), (1, 1, 0), (1, 3, 0),
    (0, 1, 1), (0, 3, 1), (1, 0, 1), (1, 2, 1), (0, 2, 1), (1, 1, 1), (1, 3, 1), (0, 0, 1),
]


def place(zl, y, core, zh, x):
    return (zl * 8 + y * 2 + core, zh * 4 + x)


def iota(shape, dim):
    return lax.broadcasted_iota(I32, shape, dim).astype(F32)


def to_column(row):
    eye = iota((128, 128), 0) == iota((128, 128), 1)
    return jnp.sum(jnp.where(eye, row, 0.0), axis=1, keepdims=True)


def ranks_of(sizes):
    column = to_column(sizes)[:16]
    ahead = jnp.logical_or(
        column < sizes,
        jnp.logical_and(column == sizes, iota((16, 128), 0) < iota((16, 128), 1)),
    )
    return jnp.sum(jnp.where(ahead, 1.0, 0.0), axis=0, keepdims=True)


def ends_column(sizes):
    upto = iota((16, 128), 1) <= iota((16, 128), 0)
    return jnp.sum(jnp.where(upto, sizes, 0.0), axis=1, keepdims=True)


def aggregates(sizes):
    ends = ends_column(sizes)
    return jnp.sum(jnp.where(ends <= iota((16, 128), 1), 1.0, 0.0), axis=0, keepdims=True)


def plan(own_sizes, low_sizes, high_sizes, local_cols):
    owner = aggregates(own_sizes)
    rank_column = to_column(ranks_of(own_sizes))[:16]
    row_rank = jnp.sum(
        jnp.where(iota((16, 128), 0) == owner, rank_column, 0.0), axis=0, keepdims=True
    )
    low, high = aggregates(low_sizes), aggregates(high_sizes) + 16.0
    low_column, high_column = to_column(low), to_column(high)
    codes = []
    for s in range(4):
        j = local_cols[s]
        target = jnp.sum(
            jnp.where(iota((128, 128), 0) == j, low_column, 0.0)
            + jnp.where(iota((128, 128), 0) + 128.0 == j, high_column, 0.0),
            axis=0, keepdims=True,
        )
        key = row_rank * 32.0 + target
        codes.append(key * 512.0 + (iota((1, 128), 1) + 128.0 * s))
    columns = [to_column(code) for code in codes]
    places = []
    for s in range(4):
        places.append(sum(
            jnp.sum(jnp.where(column < codes[s], 1.0, 0.0), axis=0, keepdims=True)
            for column in columns
        ))
    place_columns = [to_column(p) for p in places]
    order, last = [], []
    for s in range(4):
        n = iota((128, 128), 1) + 128.0 * s
        order.append(sum(
            jnp.sum(jnp.where(place_columns[q] == n, columns[q], 0.0), axis=0, keepdims=True)
            for q in range(4)
        ))
        upto = [
            sum(
                jnp.sum(jnp.where(column < (n + extra) * 512.0, 1.0, 0.0), axis=0, keepdims=True)
                for column in columns
            )
            for extra in (0.0, 1.0)
        ]
        last.append(jnp.where(upto[1] > upto[0], upto[1] - 1.0, float(TILES)))
    return order, last, [low, high]


def fused_kernel(p_hbm, s_hbm, cols_hbm, a_hbm, got, ranks_out,
                 p_in, s_in, cols_v, cols_s, sizes, mine, col_p, row_p, a_in, mid,
                 table, left, seq, running, parts, meta_v, meta_s, ranks_v,
                 in_sem, send_sem, col_sem, row_sem, size_send, size_sem, local_sem, a_sem,
                 meta_sem, part_send, part_sem):
    row = lax.axis_index("row")
    col = lax.axis_index("col")
    zl, y, core = row // 8, (row // 2) % 4, row % 2
    zh, x = col // 4, col % 4

    sibling = place(zl, y, 1 - core, zh, x)
    partner = place(1 - zl, y, core, zh, x)
    along_y = [place(zl, (y + d) % 4, core, zh, x) for d in (1, 3, 2)]
    across = place(zl, y, core, 1 - zh, x)
    along_x = [place(zl, y, core, zh, (x + d) % 4) for d in (1, 3, 2)]
    peers = [place((zl + a) % 2, (y + b) % 4, (core + c) % 2, zh, x) for a, b, c in ORDER]
    to = place(zh, x, zl, core, y)
    source = place(core, x, zh, zl, y)
    stays = jnp.logical_and(to[0] == row, to[1] == col)
    moves = jnp.logical_not(stays)

    inputs = [
        pltpu.make_async_copy(s_hbm, s_in, in_sem.at[0]),
        pltpu.make_async_copy(p_hbm, p_in, in_sem.at[1]),
        pltpu.make_async_copy(cols_hbm, cols_v, in_sem.at[2]),
        pltpu.make_async_copy(cols_hbm, cols_s, in_sem.at[3]),
    ]
    for copy in inputs:
        copy.start()

    def a_copy(k):
        return pltpu.make_async_copy(
            a_hbm.at[:, pl.ds(8 * k, 8)], a_in.at[:, pl.ds(8 * k, 8)], a_sem.at[k]
        )

    for k in range(8):
        a_copy(k).start()

    barrier = pltpu.get_barrier_semaphore()
    for there in [*peers, across, *along_x]:
        pl.semaphore_signal(barrier, 1, device_id=there, device_id_type=MESH)

    @pl.when(moves)
    def _():
        pl.semaphore_signal(barrier, 1, device_id=source, device_id_type=MESH)

    inputs[0].wait()
    s_row = jnp.zeros((8, 128), I32)
    sizes[pl.ds(row, 1)] = s_row[None]
    sizes[row, 0:1, 0:16] = s_in[...]
    inputs[1].wait()
    for k in range(8):
        mine[pl.ds(64 * k, 64), :] = jnp.concatenate([p_in[2 * k], p_in[2 * k + 1]], axis=-1)

    pl.semaphore_wait(barrier, 19 + jnp.where(stays, 0, 1))

    count = [0]
    sent = []

    def send(src, dst, sem, there):
        k = count[0]
        count[0] += 1
        copy = pltpu.make_async_remote_copy(
            src_ref=src, dst_ref=dst, send_sem=send_sem.at[k], recv_sem=sem,
            device_id=there, device_id_type=MESH,
        )
        copy.start()
        sent.append(copy)

    def arrived(ref, sem):
        pltpu.make_async_copy(ref, ref, sem).wait()

    def row_of(a, b, c):
        return a * 8 + b * 2 + c

    held = 2 * x + zh
    first = pltpu.make_async_remote_copy(
        src_ref=mine, dst_ref=row_p.at[2 * y + core],
        send_sem=send_sem.at[24], recv_sem=row_sem.at[2 * y + core],
        device_id=to, device_id_type=MESH,
    )
    first_here = pltpu.make_async_copy(mine, row_p.at[2 * y + core], row_sem.at[2 * y + core])

    @pl.when(moves)
    def _():
        first.start()

    @pl.when(stays)
    def _():
        first_here.start()

    for there in peers:
        pltpu.make_async_remote_copy(
            src_ref=sizes.at[row], dst_ref=sizes.at[row], send_sem=size_send, recv_sem=size_sem,
            device_id=there, device_id_type=MESH,
        ).start()

    for there in [partner, *along_y, sibling]:
        send(mine, col_p.at[row], col_sem.at[row], there)
    own = pltpu.make_async_copy(mine, col_p.at[row], local_sem)
    own.start()

    eye = (iota((128, 128), 0) == iota((128, 128), 1)).astype(BF)

    def turn(k):
        a_copy(k).wait()

        @pl.loop(0, 8, unroll=2)
        def _(n):
            u = 8 * k + n
            wide = jnp.concatenate([a_in[s, u] for s in range(4)], axis=0)
            tiles = lax.dot_general(eye, wide, (((1,), (1,)), ((), ())), preferred_element_type=F32)
            for h in range(2):
                at = pl.multiple_of(PITCH * (64 * h + u), 8)
                mid[pl.ds(at, 128), :] = tiles[:, 128 * h:128 * h + 128]

    lane = lax.broadcasted_iota(I32, (64, 128), 1) // 64
    zero = jnp.zeros((64, 128), BF)

    def tabulate(src):
        @pl.loop(0, 8, unroll=4)
        def _(k):
            pair = col_p[src, pl.ds(pl.multiple_of(64 * k, 64), 64), :]
            turned = jnp.concatenate([pair[:, 64:], pair[:, :64]], axis=-1)
            for h in range(2):
                j = 16 * src + 2 * k + h
                right = meta_s[8 + (j >> 7), j & 127] & 1
                table[j] = jnp.where(lane == right, jnp.where(right == h, pair, turned), zero)

    def flip(slot):
        @pl.loop(0, 8, unroll=4)
        def _(k):
            pair = row_p[slot, pl.ds(pl.multiple_of(64 * k, 64), 64), :].T
            left[16 * slot + 2 * k] = pair[:64]
            left[16 * slot + 2 * k + 1] = pair[64:]

    turn(0)

    inputs[2].wait()
    inputs[3].wait()
    pltpu.make_async_copy(sizes.at[pl.ds(0, 15)], sizes.at[pl.ds(0, 15)], size_sem).wait()
    pltpu.make_async_copy(sizes.at[pl.ds(0, 15)], sizes.at[pl.ds(0, 15)], size_send).wait()

    def sizes_of(index):
        return sizes[index, 0:1, :].astype(F32)

    order, last, halves = plan(
        sizes_of(row), sizes_of(2 * col), sizes_of(2 * col + 1),
        [(cols_v[s:s + 1, :] & 255).astype(F32) for s in range(4)],
    )
    for k in range(4):
        meta_v[k:k + 1, :] = order[k].astype(I32)
        meta_v[4 + k:5 + k, :] = last[k].astype(I32)
    for k in range(2):
        meta_v[8 + k:9 + k, :] = halves[k].astype(I32)
    to_scalars = pltpu.make_async_copy(meta_v, meta_s, meta_sem)
    to_scalars.start()

    other = row_of(1 - zl, y, core)
    arrived(col_p.at[other], col_sem.at[other])
    for there in [*along_y, sibling]:
        send(col_p.at[other], col_p.at[other], col_sem.at[other], there)
    arrived(row_p.at[held], row_sem.at[held])
    for there in [across, *along_x]:
        send(row_p.at[held], row_p.at[held], row_sem.at[held], there)

    turn(1)
    turn(2)

    across_held = 2 * x + 1 - zh
    arrived(row_p.at[across_held], row_sem.at[across_held])
    for there in along_x:
        send(row_p.at[across_held], row_p.at[across_held], row_sem.at[across_held], there)

    turn(3)
    turn(4)
    to_scalars.wait()
    own.wait()
    tabulate(row)
    tabulate(other)
    for a, h in ((zl, 0), (1 - zl, 1)):
        for d in (1, 3, 2):
            index = row_of(a, (y + d) % 4, core)
            arrived(col_p.at[index], col_sem.at[index])
            send(col_p.at[index], col_p.at[index], col_sem.at[index], sibling)
        turn(5 + h)
    turn(7)
    flip(held)
    flip(across_held)
    for a in (zl, 1 - zl):
        for d in (1, 3, 2):
            tabulate(row_of(a, (y + d) % 4, core))
    for d in (1, 3, 2):
        for h in (0, 1):
            index = 2 * ((x + d) % 4) + h
            arrived(row_p.at[index], row_sem.at[index])
            flip(index)

    @pl.loop(0, ROWS)
    def _(k):
        ranks_v[pl.ds(k, 1), :] = ranks_of(sizes_of(k)).astype(I32)

    ranks_copy = pltpu.make_async_copy(ranks_v, ranks_out, local_sem)
    ranks_copy.start()
    for a in (zl, 1 - zl):
        for d in (0, 1, 3, 2):
            index = row_of(a, (y + d) % 4, 1 - core)
            arrived(col_p.at[index], col_sem.at[index])
            tabulate(index)

    seq[TILES] = zero
    running[...] = jnp.zeros((64, 128), F32)

    def exchange_copy(there, q):
        return pltpu.make_async_remote_copy(
            src_ref=parts.at[there[0], pl.ds(2 * q, 2)],
            dst_ref=got.at[row, pl.ds(2 * q, 2)],
            send_sem=part_send.at[there[0]],
            recv_sem=part_sem.at[row],
            device_id=there,
            device_id_type=MESH,
        )

    @pl.loop(0, 8)
    def _(q):
        @pl.loop(0, 64 // GROUP)
        def _(m):
            start = 64 * q + GROUP * m
            before = jnp.maximum(start - 1, 0)
            previous = jnp.where(start == 0, -1, meta_s[before >> 7, before & 127] >> 9)
            rows, products, keeps = [], [], []
            for g in range(GROUP):
                n = start + g
                code = meta_s[n >> 7, n & 127]
                key = code >> 9
                keeps.append(key == previous)
                previous = key
                s = (code >> 7) & 3
                i = code & 127
                rows.append(i)
                j = cols_s[s, i] & 255
                tile = mid[pl.ds((s >> 1) * (64 * PITCH) + i, 64, stride=PITCH), :]
                tile = jnp.where(lane == (s & 1), tile, 0.0).astype(BF)
                right = table[j]
                products.append(
                    jnp.dot(
                        tile, jnp.concatenate([right, right], axis=0), preferred_element_type=F32
                    ).astype(BF)
                )
            pieces = [
                jnp.dot(left[rows[g]], products[g], preferred_element_type=F32)
                for g in range(GROUP)
            ]
            total = running[...]
            for g in range(GROUP):
                total = pieces[g] + jnp.where(keeps[g], total, 0.0)
                seq[start + g] = total.astype(BF)
            running[...] = total

        @pl.loop(0, ROWS, unroll=2)
        def _(d):
            for h in range(2):
                key = (2 * q + h) * 32 + 2 * d
                one = jnp.clip(meta_s[4 + (key >> 7), key & 127], 0, TILES)
                two = jnp.clip(meta_s[4 + (key >> 7), (key & 127) + 1], 0, TILES)
                parts[d, 2 * q + h] = jnp.where(lane == 0, seq[one], seq[two])

        for there in peers:
            exchange_copy(there, q).start()

    mine_copy = pltpu.make_async_copy(parts.at[row], got.at[row], part_send.at[row])
    mine_copy.start()

    @pl.when(moves)
    def _():
        first.wait_send()

    for copy in sent:
        copy.wait_send()
    ranks_copy.wait()
    mine_copy.wait()
    for there in peers:
        arrived(parts.at[there[0]], part_send.at[there[0]])
        arrived(got.at[there[0]], part_sem.at[there[0]])


def fused(p_tiles, sizes, a_cols, a_turned):
    hbm = pl.BlockSpec(memory_space=pltpu.HBM)
    free = pl.BlockSpec(memory_space=pl.ANY)
    dma = pltpu.SemaphoreType.DMA
    return pl.pallas_call(
        fused_kernel,
        out_shape=(
            jax.ShapeDtypeStruct((ROWS, 16, 64, 128), BF),
            jax.ShapeDtypeStruct((ROWS, 128), I32),
        ),
        in_specs=[hbm] * 4,
        out_specs=[free, free],
        scratch_shapes=[
            pltpu.VMEM((16, 64, 64), BF),
            pltpu.VMEM((1, 16), I32),
            pltpu.VMEM((4, 128), I32),
            pltpu.SMEM((4, 128), I32),
            pltpu.VMEM((ROWS, 8, 128), I32),
            pltpu.VMEM((512, 128), BF),
            pltpu.VMEM((ROWS, 512, 128), BF),
            pltpu.VMEM((8, 512, 128), BF),
            pltpu.VMEM((4, 64, 64, 128), BF),
            pltpu.VMEM((128 * PITCH, 128), F32),
            pltpu.VMEM((256, 64, 128), BF),
            pltpu.VMEM((128, 64, 64), BF),
            pltpu.VMEM((TILES + 1, 64, 128), BF),
            pltpu.VMEM((64, 128), F32),
            pltpu.VMEM((ROWS, 16, 64, 128), BF),
            pltpu.VMEM((16, 128), I32),
            pltpu.SMEM((16, 128), I32),
            pltpu.VMEM((ROWS, 128), I32),
            dma((4,)),
            dma((25,)),
            dma((ROWS,)),
            dma((8,)),
            dma,
            dma,
            dma,
            dma((8,)),
            dma,
            dma((ROWS,)),
            dma((ROWS,)),
        ],
        compiler_params=pltpu.CompilerParams(
            collective_id=0, has_side_effects=True, vmem_limit_bytes=48 * MIB
        ),
    )(p_tiles, sizes, a_cols, a_turned)


def widen_kernel(ranks, got, out_hbm, wide, sem):
    def copy(k):
        return pltpu.make_async_copy(wide.at[k % 4], out_hbm.at[pl.ds(16 * k, 16)], sem.at[k % 4])

    for k in range(ROWS):
        if k >= 4:
            copy(k - 4).wait()

        @pl.loop(0, 16, unroll=2)
        def _(a):
            wide[k % 4, a] = got[k, ranks[k, a]].astype(F32)

        copy(k).start()
    for k in range(ROWS - 4, ROWS):
        copy(k).wait()


def widen(ranks, got):
    return pl.pallas_call(
        widen_kernel,
        out_shape=jax.ShapeDtypeStruct((256, 64, 128), F32),
        in_specs=[
            pl.BlockSpec(memory_space=pltpu.SMEM),
            pl.BlockSpec(memory_space=pltpu.VMEM),
        ],
        out_specs=pl.BlockSpec(memory_space=pltpu.HBM),
        scratch_shapes=[pltpu.VMEM((4, 16, 64, 128), F32), pltpu.SemaphoreType.DMA((4,))],
        compiler_params=pltpu.CompilerParams(vmem_limit_bytes=12 * MIB),
    )(ranks, got)


def per_device(a_tiles, a_cols, p_tiles, agg_sizes):
    got, ranks = fused(p_tiles, agg_sizes, a_cols.T, a_tiles.transpose(1, 2, 3, 0))
    return widen(ranks, got)


def solution(mesh):
    return jax.shard_map(
        per_device,
        mesh=mesh,
        in_specs=(
            P("row", "col", None, None),
            P("row", "col"),
            P(("col", "row"), None, None),
            P("row", None),
        ),
        out_specs=P(None, None, ("col", "row")),
        check_vma=False,
    )
```

```python
import jax
import jax.numpy as jnp
from jax import lax
from jax.experimental import pallas as pl
from jax.experimental.pallas import tpu as pltpu
from jax.sharding import PartitionSpec as P

MESH = pl.DeviceIdType.MESH
ROWS = 16
COLS = 8
MIB = 1 << 20
PITCH = 136
TILES = 512
GROUP = 16
BF = jnp.bfloat16
F32 = jnp.float32
I32 = jnp.int32

ORDER = [
    (0, 1, 0), (0, 3, 0), (1, 0, 0), (1, 2, 0), (0, 2, 0), (1, 1, 0), (1, 3, 0),
    (0, 1, 1), (0, 3, 1), (1, 0, 1), (1, 2, 1), (0, 2, 1), (1, 1, 1), (1, 3, 1), (0, 0, 1),
]


def place(zl, y, core, zh, x):
    return (zl * 8 + y * 2 + core, zh * 4 + x)


def iota(shape, dim):
    return lax.broadcasted_iota(I32, shape, dim).astype(F32)


def to_column(row):
    eye = iota((128, 128), 0) == iota((128, 128), 1)
    return jnp.sum(jnp.where(eye, row, 0.0), axis=1, keepdims=True)


def ranks_of(sizes):
    column = to_column(sizes)[:16]
    ahead = jnp.logical_or(
        column < sizes,
        jnp.logical_and(column == sizes, iota((16, 128), 0) < iota((16, 128), 1)),
    )
    return jnp.sum(jnp.where(ahead, 1.0, 0.0), axis=0, keepdims=True)


def ends_column(sizes):
    upto = iota((16, 128), 1) <= iota((16, 128), 0)
    return jnp.sum(jnp.where(upto, sizes, 0.0), axis=1, keepdims=True)


def aggregates(sizes):
    ends = ends_column(sizes)
    return jnp.sum(jnp.where(ends <= iota((16, 128), 1), 1.0, 0.0), axis=0, keepdims=True)


def plan(own_sizes, low_sizes, high_sizes, local_cols):
    owner = aggregates(own_sizes)
    rank_column = to_column(ranks_of(own_sizes))[:16]
    row_rank = jnp.sum(
        jnp.where(iota((16, 128), 0) == owner, rank_column, 0.0), axis=0, keepdims=True
    )
    low, high = aggregates(low_sizes), aggregates(high_sizes) + 16.0
    low_column, high_column = to_column(low), to_column(high)
    codes = []
    for s in range(4):
        j = local_cols[s]
        target = jnp.sum(
            jnp.where(iota((128, 128), 0) == j, low_column, 0.0)
            + jnp.where(iota((128, 128), 0) + 128.0 == j, high_column, 0.0),
            axis=0, keepdims=True,
        )
        key = row_rank * 32.0 + target
        codes.append(key * 512.0 + (iota((1, 128), 1) + 128.0 * s))
    columns = [to_column(code) for code in codes]
    places = []
    for s in range(4):
        places.append(sum(
            jnp.sum(jnp.where(column < codes[s], 1.0, 0.0), axis=0, keepdims=True)
            for column in columns
        ))
    place_columns = [to_column(p) for p in places]
    order, last = [], []
    for s in range(4):
        n = iota((128, 128), 1) + 128.0 * s
        order.append(sum(
            jnp.sum(jnp.where(place_columns[q] == n, columns[q], 0.0), axis=0, keepdims=True)
            for q in range(4)
        ))
        upto = [
            sum(
                jnp.sum(jnp.where(column < (n + extra) * 512.0, 1.0, 0.0), axis=0, keepdims=True)
                for column in columns
            )
            for extra in (0.0, 1.0)
        ]
        last.append(jnp.where(upto[1] > upto[0], upto[1] - 1.0, float(TILES)))
    return order, last, [low, high]


def fused_kernel(p_hbm, s_hbm, cols_hbm, a_hbm, got, ranks_out,
                 p_in, s_in, cols_v, cols_s, sizes, mine, mine_left, col_p, row_p, a_in, mid, a_buf,
                 table, left, products, seq, running, parts, meta_v, meta_s, ranks_v,
                 in_sem, send_sem, col_sem, row_sem, first_sem, size_send, size_sem, local_sem, a_sem,
                 meta_sem, part_send, part_sem):
    row = lax.axis_index("row")
    col = lax.axis_index("col")
    zl, y, core = row // 8, (row // 2) % 4, row % 2
    zh, x = col // 4, col % 4

    sibling = place(zl, y, 1 - core, zh, x)
    partner = place(1 - zl, y, core, zh, x)
    along_y = [place(zl, (y + d) % 4, core, zh, x) for d in (1, 3)]
    across = place(zl, y, core, 1 - zh, x)
    along_x = [place(zl, y, core, zh, (x + d) % 4) for d in (1, 3)]
    peers = [place((zl + a) % 2, (y + b) % 4, (core + c) % 2, zh, x) for a, b, c in ORDER]
    to = place(zh, x, zl, core, (x + y) % 4)
    source = place(core, (x - y + 4) % 4, zh, zl, y)
    stays = jnp.logical_and(to[0] == row, to[1] == col)
    moves = jnp.logical_not(stays)

    inputs = [
        pltpu.make_async_copy(s_hbm, s_in, in_sem.at[0]),
        pltpu.make_async_copy(p_hbm, p_in, in_sem.at[1]),
        pltpu.make_async_copy(cols_hbm, cols_v, in_sem.at[2]),
        pltpu.make_async_copy(cols_hbm, cols_s, in_sem.at[3]),
    ]
    for copy in inputs:
        copy.start()

    def a_copy(k):
        return pltpu.make_async_copy(
            a_hbm.at[:, pl.ds(8 * k, 8)], a_in.at[:, pl.ds(8 * k, 8)], a_sem.at[k]
        )

    for k in range(8):
        a_copy(k).start()

    barrier = pltpu.get_barrier_semaphore()
    for there in [*peers, across, *along_x]:
        pl.semaphore_signal(barrier, 1, device_id=there, device_id_type=MESH)

    @pl.when(moves)
    def _():
        pl.semaphore_signal(barrier, 1, device_id=source, device_id_type=MESH)

    inputs[0].wait()
    s_row = jnp.zeros((8, 128), I32)
    sizes[pl.ds(row, 1)] = s_row[None]
    sizes[row, 0:1, 0:16] = s_in[...]
    inputs[1].wait()
    for k in range(8):
        mine[pl.ds(64 * k, 64), :] = jnp.concatenate([p_in[2 * k], p_in[2 * k + 1]], axis=-1)
    for h in range(2):
        for k in range(4):
            mine_left[h, pl.ds(64 * k, 64), :] = jnp.concatenate(
                [p_in[4 * k + n][:, 32 * h:32 * h + 32] for n in range(4)], axis=-1
            )

    pl.semaphore_wait(barrier, 18 + jnp.where(stays, 0, 1))

    count = [0]
    sent = []

    def send(src, dst, sem, there):
        k = count[0]
        count[0] += 1
        copy = pltpu.make_async_remote_copy(
            src_ref=src, dst_ref=dst, send_sem=send_sem.at[k], recv_sem=sem,
            device_id=there, device_id_type=MESH,
        )
        copy.start()
        sent.append(copy)

    def arrived(ref, sem):
        pltpu.make_async_copy(ref, ref, sem).wait()

    def row_of(a, b, c):
        return a * 8 + b * 2 + c

    def slot_at(x, h):
        return 2 * ((x - y + 4) % 4) + h

    held, across_held = slot_at(x, zh), slot_at(x, 1 - zh)

    def first(u):
        return pltpu.make_async_remote_copy(
            src_ref=mine_left.at[u], dst_ref=row_p.at[u, 2 * y + core],
            send_sem=first_sem.at[u], recv_sem=row_sem.at[u, 2 * y + core],
            device_id=to, device_id_type=MESH,
        )

    def first_step(u):
        @pl.when(moves)
        def _():
            first(u).start()

        @pl.when(stays)
        def _():
            pltpu.make_async_copy(
                mine_left.at[u], row_p.at[u, 2 * y + core], row_sem.at[u, 2 * y + core]
            ).start()

    first_step(0)

    for there in peers:
        pltpu.make_async_remote_copy(
            src_ref=sizes.at[row], dst_ref=sizes.at[row], send_sem=size_send, recv_sem=size_sem,
            device_id=there, device_id_type=MESH,
        ).start()

    def col_send(index, there, half=None):
        rows = pl.ds(0, 512) if half is None else pl.ds(256 * half, 256)
        ref = col_p.at[index, rows]
        send(mine if index is row else ref, ref, col_sem.at[index], there)

    def row_send(u, slot, there, half=None):
        rows = pl.ds(0, 256) if half is None else pl.ds(128 * half, 128)
        ref = row_p.at[u, slot, rows]
        send(ref, ref, row_sem.at[u, slot], there)

    def row_arrived(u, slot):
        arrived(row_p.at[u, slot], row_sem.at[u, slot])

    right_y, left_y = along_y
    right_x, left_x = along_x
    for there in (partner, right_y, left_y, sibling):
        col_send(row, there)
    own = pltpu.make_async_copy(mine, col_p.at[row], local_sem)
    own.start()

    def turn(k):
        a_copy(k).wait()

        @pl.loop(0, 8, unroll=2)
        def _(n):
            u = 8 * k + n
            wide = jnp.concatenate([a_in[s, u] for s in range(4)], axis=0)
            tiles = wide.T.astype(F32)
            for h in range(2):
                at = pl.multiple_of(PITCH * (64 * h + u), 8)
                mid[pl.ds(at, 128), :] = tiles[:, 128 * h:128 * h + 128]

    def pick(k):
        @pl.loop(0, 16, unroll=4)
        def _(n):
            i = 16 * k + n
            for h in range(2):
                both = mid[pl.ds(64 * PITCH * h + i, 64, stride=PITCH), :]
                a_buf[256 * h + i] = both[:, :64].astype(BF)
                a_buf[256 * h + 128 + i] = pltpu.roll(both, 64, 1)[:, :64].astype(BF)

    lane = lax.broadcasted_iota(I32, (64, 128), 1) // 64

    def flip(u, slot):
        for k in range(4):
            turned = row_p[u, slot, 64 * k:64 * k + 64, :].T
            for n in range(4):
                left[u, 16 * slot + 4 * k + n] = turned[32 * n:32 * n + 32]

    zero = jnp.zeros((64, 128), BF)

    def tabulate(src):
        @pl.loop(0, 8, unroll=4)
        def _(k):
            pair = col_p[src, pl.ds(pl.multiple_of(64 * k, 64), 64), :]
            turned = jnp.concatenate([pair[:, 64:], pair[:, :64]], axis=-1)
            for h in range(2):
                j = 16 * src + 2 * k + h
                right = meta_s[8 + (j >> 7), j & 127] & 1
                table[j] = jnp.where(lane == right, jnp.where(right == h, pair, turned), zero)

    turn(0)
    turn(1)

    row_arrived(0, held)
    row_send(0, held, right_x)
    row_send(0, held, left_x)
    row_send(0, held, across)
    other = row_of(1 - zl, y, core)
    arrived(col_p.at[other], col_sem.at[other])
    col_send(other, right_y)
    col_send(other, left_y)
    col_send(other, sibling)

    before_x, after_x = (x + 3) % 4, (x + 1) % 4
    before_y, after_y = (y + 3) % 4, (y + 1) % 4
    row_arrived(0, across_held)
    row_send(0, across_held, right_x)
    row_send(0, across_held, left_x)

    def row_relay(u, h):
        for where, half, there in ((before_x, 0, right_x), (after_x, 1, left_x)):
            row_arrived(u, slot_at(where, h))
            row_send(u, slot_at(where, h), there, half)

    def col_relay(a):
        for where, half, there in ((before_y, 0, right_y), (after_y, 1, left_y)):
            index = row_of(a, where, core)
            arrived(col_p.at[index], col_sem.at[index])
            col_send(index, there, half)
            col_send(index, sibling)

    for k in range(2, 6):
        turn(k)
    row_relay(0, zh)
    col_relay(zl)
    turn(6)
    turn(7)
    inputs[2].wait()
    inputs[3].wait()
    pltpu.make_async_copy(sizes.at[pl.ds(0, 15)], sizes.at[pl.ds(0, 15)], size_sem).wait()
    pltpu.make_async_copy(sizes.at[pl.ds(0, 15)], sizes.at[pl.ds(0, 15)], size_send).wait()

    def sizes_of(index):
        return sizes[index, 0:1, :].astype(F32)

    order, last, halves = plan(
        sizes_of(row), sizes_of(2 * col), sizes_of(2 * col + 1),
        [(cols_v[s:s + 1, :] & 255).astype(F32) for s in range(4)],
    )
    for k in range(4):
        meta_v[k:k + 1, :] = order[k].astype(I32)
        meta_v[4 + k:5 + k, :] = last[k].astype(I32)
    for k in range(2):
        meta_v[8 + k:9 + k, :] = halves[k].astype(I32)
    to_scalars = pltpu.make_async_copy(meta_v, meta_s, meta_sem)
    to_scalars.start()

    row_relay(0, 1 - zh)
    col_relay(1 - zl)
    first_step(1)
    pick(0)
    pick(1)
    for a in (zl, 1 - zl):
        index = row_of(a, (y + 2) % 4, core)
        arrived(col_p.at[index], col_sem.at[index])
        col_send(index, sibling)
    pick(2)
    pick(3)
    to_scalars.wait()
    own.wait()
    for slot in (held, across_held, *[slot_at(w, h) for w in (before_x, after_x) for h in (0, 1)]):
        flip(0, slot)
    for k in range(4, 8):
        pick(k)
    for a in (zl, 1 - zl):
        for d in range(4):
            tabulate(row_of(a, (y + d) % 4, core))

    for h in (zh, 1 - zh):
        slot = slot_at((x + 2) % 4, h)
        row_arrived(0, slot)
        flip(0, slot)
    for a in (zl, 1 - zl):
        for d in (0, 1, 3, 2):
            index = row_of(a, (y + d) % 4, 1 - core)
            arrived(col_p.at[index], col_sem.at[index])
            tabulate(index)

    seq[TILES] = jnp.zeros((32, 128), BF)
    running[...] = jnp.zeros((32, 128), F32)

    def exchange_copy(there, u, q):
        return pltpu.make_async_remote_copy(
            src_ref=parts.at[there[0], u, pl.ds(2 * q, 2)],
            dst_ref=got.at[row, u, pl.ds(2 * q, 2)],
            send_sem=part_send.at[there[0]],
            recv_sem=part_sem.at[row],
            device_id=there,
            device_id_type=MESH,
        )

    def chunks(u, begin, end):
        @pl.loop(begin, end)
        def _(q):
            @pl.loop(0, 64 // GROUP)
            def _(m):
                start = 64 * q + GROUP * m
                before = jnp.maximum(start - 1, 0)
                previous = jnp.where(start == 0, -1, meta_s[before >> 7, before & 127] >> 9)
                rows, keeps, rights = [], [], []
                for g in range(GROUP):
                    n = start + g
                    code = meta_s[n >> 7, n & 127]
                    key = code >> 9
                    keeps.append(key == previous)
                    previous = key
                    i = code & 127
                    rows.append(i)
                    if u == 0:
                        j = cols_s[(code >> 7) & 3, i] & 255
                        rights.append(
                            jnp.dot(
                                a_buf[code & 511], table[j], preferred_element_type=F32
                            ).astype(BF)
                        )
                        products[n] = rights[g]
                    else:
                        rights.append(products[n])
                pieces = [
                    jnp.dot(left[u, rows[g]], rights[g], preferred_element_type=F32)
                    for g in range(GROUP)
                ]
                total = running[...]
                for g in range(GROUP):
                    total = pieces[g] + jnp.where(keeps[g], total, 0.0)
                    seq[start + g] = total.astype(BF)
                running[...] = total

            @pl.loop(0, ROWS, unroll=4)
            def _(d):
                for h in range(2):
                    key = 64 * q + 32 * h + 2 * d
                    one = jnp.clip(meta_s[4 + (key >> 7), key & 127], 0, TILES)
                    two = jnp.clip(meta_s[4 + (key >> 7), (key & 127) + 1], 0, TILES)
                    parts[d, u, 2 * q + h] = jnp.where(lane[:32] == 0, seq[one], seq[two])

            for there in peers:
                exchange_copy(there, u, q).start()

    chunks(0, 0, 1)
    row_arrived(1, held)
    row_send(1, held, right_x)
    row_send(1, held, left_x)
    row_send(1, held, across)
    chunks(0, 1, 3)
    @pl.loop(0, ROWS)
    def _(k):
        ranks_v[pl.ds(k, 1), :] = ranks_of(sizes_of(k)).astype(I32)

    ranks_copy = pltpu.make_async_copy(ranks_v, ranks_out, local_sem)
    ranks_copy.start()
    row_arrived(1, across_held)
    row_send(1, across_held, right_x)
    row_send(1, across_held, left_x)
    row_relay(1, zh)
    chunks(0, 3, 5)
    row_relay(1, 1 - zh)
    chunks(0, 5, 8)
    for h in (zh, 1 - zh):
        row_arrived(1, slot_at((x + 2) % 4, h))
    for slot in range(8):
        flip(1, slot)
    chunks(1, 0, 8)

    mine_copy = pltpu.make_async_copy(parts.at[row], got.at[row], part_send.at[row])
    mine_copy.start()

    @pl.when(moves)
    def _():
        first(0).wait_send()
        first(1).wait_send()

    for copy in sent:
        copy.wait_send()
    ranks_copy.wait()
    mine_copy.wait()
    for there in peers:
        arrived(parts.at[there[0]], part_send.at[there[0]])
        arrived(got.at[there[0]], part_sem.at[there[0]])


def fused(p_tiles, sizes, a_cols, a_turned):
    hbm = pl.BlockSpec(memory_space=pltpu.HBM)
    free = pl.BlockSpec(memory_space=pl.ANY)
    dma = pltpu.SemaphoreType.DMA
    return pl.pallas_call(
        fused_kernel,
        out_shape=(
            jax.ShapeDtypeStruct((ROWS, 2, 16, 32, 128), BF),
            jax.ShapeDtypeStruct((ROWS, 128), I32),
        ),
        in_specs=[hbm] * 4,
        out_specs=[free, free],
        scratch_shapes=[
            pltpu.VMEM((16, 64, 64), BF),
            pltpu.VMEM((1, 16), I32),
            pltpu.VMEM((4, 128), I32),
            pltpu.SMEM((4, 128), I32),
            pltpu.VMEM((ROWS, 8, 128), I32),
            pltpu.VMEM((512, 128), BF),
            pltpu.VMEM((2, 256, 128), BF),
            pltpu.VMEM((ROWS, 512, 128), BF),
            pltpu.VMEM((2, 8, 256, 128), BF),
            pltpu.VMEM((4, 64, 64, 128), BF),
            pltpu.VMEM((128 * PITCH, 128), F32),
            pltpu.VMEM((TILES, 64, 64), BF),
            pltpu.VMEM((256, 64, 128), BF),
            pltpu.VMEM((2, 128, 32, 64), BF),
            pltpu.VMEM((TILES, 64, 128), BF),
            pltpu.VMEM((TILES + 1, 32, 128), BF),
            pltpu.VMEM((32, 128), F32),
            pltpu.VMEM((ROWS, 2, 16, 32, 128), BF),
            pltpu.VMEM((16, 128), I32),
            pltpu.SMEM((16, 128), I32),
            pltpu.VMEM((ROWS, 128), I32),
            dma((4,)),
            dma((35,)),
            dma((ROWS,)),
            dma((2, 8)),
            dma((2,)),
            dma,
            dma,
            dma,
            dma((8,)),
            dma,
            dma((ROWS,)),
            dma((ROWS,)),
        ],
        compiler_params=pltpu.CompilerParams(
            collective_id=0, has_side_effects=True, vmem_limit_bytes=58 * MIB
        ),
    )(p_tiles, sizes, a_cols, a_turned)


def widen_kernel(ranks_hbm, got, out_hbm, ranks, narrow, wide, ranks_sem, in_sem, sem):
    def fetch(k):
        return pltpu.make_async_copy(got.at[k], narrow.at[k], in_sem.at[k])

    def copy(k):
        return pltpu.make_async_copy(wide.at[k % 8], out_hbm.at[pl.ds(16 * k, 16)], sem.at[k % 8])

    ranks_copy = pltpu.make_async_copy(ranks_hbm, ranks, ranks_sem)
    ranks_copy.start()
    for k in range(ROWS):
        fetch(k).start()
    ranks_copy.wait()
    for k in range(ROWS):
        if k >= 8:
            copy(k - 8).wait()
        fetch(k).wait()

        @pl.loop(0, 16, unroll=4)
        def _(a):
            for h in range(2):
                wide[k % 8, a, 32 * h:32 * h + 32] = narrow[k, h, ranks[k, a]].astype(F32)

        copy(k).start()
    for k in range(ROWS - 8, ROWS):
        copy(k).wait()


def widen(ranks, got):
    free = pl.BlockSpec(memory_space=pl.ANY)
    return pl.pallas_call(
        widen_kernel,
        out_shape=jax.ShapeDtypeStruct((256, 64, 128), F32),
        in_specs=[free, free],
        out_specs=free,
        scratch_shapes=[
            pltpu.SMEM((ROWS, 128), I32),
            pltpu.VMEM((ROWS, 2, 16, 32, 128), BF),
            pltpu.VMEM((8, 16, 64, 128), F32),
            pltpu.SemaphoreType.DMA,
            pltpu.SemaphoreType.DMA((ROWS,)),
            pltpu.SemaphoreType.DMA((8,)),
        ],
        compiler_params=pltpu.CompilerParams(vmem_limit_bytes=58 * MIB),
    )(ranks, got)


def per_device(a_tiles, a_cols, p_tiles, agg_sizes):
    got, ranks = fused(p_tiles, agg_sizes, a_cols.T, a_tiles.transpose(1, 2, 3, 0))
    return widen(ranks, got)


def solution(mesh):
    return jax.shard_map(
        per_device,
        mesh=mesh,
        in_specs=(
            P("row", "col", None, None),
            P("row", "col"),
            P(("col", "row"), None, None),
            P("row", None),
        ),
        out_specs=P(None, None, ("col", "row")),
        check_vma=False,
    )
```

```python
import jax
import jax.numpy as jnp
from jax import lax
from jax.experimental import pallas as pl
from jax.experimental.pallas import tpu as pltpu
from jax.sharding import PartitionSpec as P

MESH = pl.DeviceIdType.MESH
ROWS = 16
COLS = 8
MIB = 1 << 20
PITCH = 136
TILES = 512
GROUP = 16
BF = jnp.bfloat16
F32 = jnp.float32
I32 = jnp.int32

ORDER = [
    (0, 1, 0), (0, 3, 0), (1, 0, 0), (1, 2, 0), (0, 2, 0), (1, 1, 0), (1, 3, 0),
    (0, 1, 1), (0, 3, 1), (1, 0, 1), (1, 2, 1), (0, 2, 1), (1, 1, 1), (1, 3, 1), (0, 0, 1),
]


def place(zl, y, core, zh, x):
    return (zl * 8 + y * 2 + core, zh * 4 + x)


def iota(shape, dim):
    return lax.broadcasted_iota(I32, shape, dim).astype(F32)


def to_column(row):
    eye = iota((128, 128), 0) == iota((128, 128), 1)
    return jnp.sum(jnp.where(eye, row, 0.0), axis=1, keepdims=True)


def ranks_of(sizes):
    column = to_column(sizes)[:16]
    ahead = jnp.logical_or(
        column < sizes,
        jnp.logical_and(column == sizes, iota((16, 128), 0) < iota((16, 128), 1)),
    )
    return jnp.sum(jnp.where(ahead, 1.0, 0.0), axis=0, keepdims=True)


def ends_column(sizes):
    upto = iota((16, 128), 1) <= iota((16, 128), 0)
    return jnp.sum(jnp.where(upto, sizes, 0.0), axis=1, keepdims=True)


def aggregates(sizes):
    ends = ends_column(sizes)
    return jnp.sum(jnp.where(ends <= iota((16, 128), 1), 1.0, 0.0), axis=0, keepdims=True)


def plan(own_sizes, low_sizes, high_sizes, local_cols):
    owner = aggregates(own_sizes)
    rank_column = to_column(ranks_of(own_sizes))[:16]
    row_rank = jnp.sum(
        jnp.where(iota((16, 128), 0) == owner, rank_column, 0.0), axis=0, keepdims=True
    )
    low_column = to_column(aggregates(low_sizes))
    high_column = to_column(aggregates(high_sizes) + 16.0)
    codes = []
    for s in range(4):
        j = local_cols[s]
        target = jnp.sum(
            jnp.where(iota((128, 128), 0) == j, low_column, 0.0)
            + jnp.where(iota((128, 128), 0) + 128.0 == j, high_column, 0.0),
            axis=0, keepdims=True,
        )
        key = row_rank * 64.0 + target * 2.0 + (j - 2.0 * jnp.floor(j * 0.5))
        codes.append(key * 512.0 + (iota((1, 128), 1) + 128.0 * s))
    columns = [to_column(code) for code in codes]
    places = []
    for s in range(4):
        places.append(sum(
            jnp.sum(jnp.where(column < codes[s], 1.0, 0.0), axis=0, keepdims=True)
            for column in columns
        ))
    place_columns = [to_column(p) for p in places]
    order, last = [], []
    for s in range(4):
        n = iota((128, 128), 1) + 128.0 * s
        order.append(sum(
            jnp.sum(jnp.where(place_columns[q] == n, columns[q], 0.0), axis=0, keepdims=True)
            for q in range(4)
        ))
    key_columns = [jnp.floor(column * (1.0 / 512.0)) for column in columns]
    for s in range(8):
        n = iota((128, 128), 1) + 128.0 * s
        at = [
            jnp.max(jnp.where(key_columns[q] == n, place_columns[q], -1.0), axis=0, keepdims=True)
            for q in range(4)
        ]
        at = jnp.maximum(jnp.maximum(at[0], at[1]), jnp.maximum(at[2], at[3]))
        last.append(jnp.where(at < 0.0, float(TILES), at))
    return order, last


def fused_kernel(p_hbm, s_hbm, cols_hbm, a_hbm, got, ranks_out,
                 p_in, s_in, cols_v, cols_s, sizes, mine, mine_left, col_p, row_p, a_in, mid, a_buf,
                 left, products, seq, running, parts, meta_v, meta_s, ranks_v,
                 in_sem, send_sem, col_sem, row_sem, first_sem, size_send, size_sem, local_sem, a_sem,
                 meta_sem, part_send, part_sem):
    row = lax.axis_index("row")
    col = lax.axis_index("col")
    zl, y, core = row // 8, (row // 2) % 4, row % 2
    zh, x = col // 4, col % 4

    sibling = place(zl, y, 1 - core, zh, x)
    partner = place(1 - zl, y, core, zh, x)
    along_y = [place(zl, (y + d) % 4, core, zh, x) for d in (1, 3)]
    across = place(zl, y, core, 1 - zh, x)
    along_x = [place(zl, y, core, zh, (x + d) % 4) for d in (1, 3)]
    peers = [place((zl + a) % 2, (y + b) % 4, (core + c) % 2, zh, x) for a, b, c in ORDER]
    to = place(zh, x, zl, core, (x + y) % 4)
    source = place(core, (x - y + 4) % 4, zh, zl, y)
    stays = jnp.logical_and(to[0] == row, to[1] == col)
    moves = jnp.logical_not(stays)

    inputs = [
        pltpu.make_async_copy(s_hbm, s_in, in_sem.at[0]),
        pltpu.make_async_copy(p_hbm, p_in, in_sem.at[1]),
        pltpu.make_async_copy(cols_hbm, cols_v, in_sem.at[2]),
        pltpu.make_async_copy(cols_hbm, cols_s, in_sem.at[3]),
    ]
    for copy in inputs:
        copy.start()

    def a_copy(k):
        return pltpu.make_async_copy(
            a_hbm.at[:, pl.ds(8 * k, 8)], a_in.at[:, pl.ds(8 * k, 8)], a_sem.at[k]
        )

    for k in range(8):
        a_copy(k).start()

    barrier = pltpu.get_barrier_semaphore()
    for there in [*peers, across, *along_x]:
        pl.semaphore_signal(barrier, 1, device_id=there, device_id_type=MESH)

    @pl.when(moves)
    def _():
        pl.semaphore_signal(barrier, 1, device_id=source, device_id_type=MESH)

    inputs[0].wait()
    s_row = jnp.zeros((8, 128), I32)
    sizes[pl.ds(row, 1)] = s_row[None]
    sizes[row, 0:1, 0:16] = s_in[...]
    inputs[1].wait()
    for k in range(8):
        mine[k] = jnp.concatenate([p_in[2 * k], p_in[2 * k + 1]], axis=-1)
    for h in range(2):
        for k in range(4):
            mine_left[h, pl.ds(64 * k, 64), :] = jnp.concatenate(
                [p_in[4 * k + n][:, 32 * h:32 * h + 32] for n in range(4)], axis=-1
            )

    pl.semaphore_wait(barrier, 18 + jnp.where(stays, 0, 1))

    count = [0]
    sent = []

    def send(src, dst, sem, there):
        k = count[0]
        count[0] += 1
        copy = pltpu.make_async_remote_copy(
            src_ref=src, dst_ref=dst, send_sem=send_sem.at[k], recv_sem=sem,
            device_id=there, device_id_type=MESH,
        )
        copy.start()
        sent.append(copy)

    def arrived(ref, sem):
        pltpu.make_async_copy(ref, ref, sem).wait()

    def row_of(a, b, c):
        return a * 8 + b * 2 + c

    def slot_at(x, h):
        return 2 * ((x - y + 4) % 4) + h

    held, across_held = slot_at(x, zh), slot_at(x, 1 - zh)

    def first(u):
        return pltpu.make_async_remote_copy(
            src_ref=mine_left.at[u], dst_ref=row_p.at[u, 2 * y + core],
            send_sem=first_sem.at[u], recv_sem=row_sem.at[u, 2 * y + core],
            device_id=to, device_id_type=MESH,
        )

    def first_step(u):
        @pl.when(moves)
        def _():
            first(u).start()

        @pl.when(stays)
        def _():
            pltpu.make_async_copy(
                mine_left.at[u], row_p.at[u, 2 * y + core], row_sem.at[u, 2 * y + core]
            ).start()

    first_step(0)

    for there in peers:
        pltpu.make_async_remote_copy(
            src_ref=sizes.at[row], dst_ref=sizes.at[row], send_sem=size_send, recv_sem=size_sem,
            device_id=there, device_id_type=MESH,
        ).start()

    def col_send(index, there, half=None):
        pairs = pl.ds(0, 8) if half is None else pl.ds(4 * half, 4)
        ref = col_p.at[index, pairs]
        send(mine if index is row else ref, ref, col_sem.at[index], there)

    def row_send(u, slot, there, half=None):
        rows = pl.ds(0, 256) if half is None else pl.ds(128 * half, 128)
        ref = row_p.at[u, slot, rows]
        send(ref, ref, row_sem.at[u, slot], there)

    def row_arrived(u, slot):
        arrived(row_p.at[u, slot], row_sem.at[u, slot])

    right_y, left_y = along_y
    right_x, left_x = along_x
    for there in (partner, right_y, left_y, sibling):
        col_send(row, there)
    own = pltpu.make_async_copy(mine, col_p.at[row], local_sem)
    own.start()

    def turn(k):
        a_copy(k).wait()

        @pl.loop(0, 8, unroll=2)
        def _(n):
            u = 8 * k + n
            wide = jnp.concatenate([a_in[s, u] for s in range(4)], axis=0)
            tiles = wide.T.astype(F32)
            for h in range(2):
                at = pl.multiple_of(PITCH * (64 * h + u), 8)
                mid[pl.ds(at, 128), :] = tiles[:, 128 * h:128 * h + 128]

    def pick(k):
        @pl.loop(0, 16, unroll=4)
        def _(n):
            i = 16 * k + n
            for h in range(2):
                both = mid[pl.ds(64 * PITCH * h + i, 64, stride=PITCH), :]
                a_buf[256 * h + i] = both[:, :64].astype(BF)
                a_buf[256 * h + 128 + i] = pltpu.roll(both, 64, 1)[:, :64].astype(BF)

    lane = lax.broadcasted_iota(I32, (64, 128), 1) // 64

    def flip(u, slot):
        for k in range(4):
            turned = row_p[u, slot, 64 * k:64 * k + 64, :].T
            for n in range(4):
                left[u, 16 * slot + 4 * k + n] = turned[32 * n:32 * n + 32]

    turn(0)
    turn(1)

    row_arrived(0, held)
    row_send(0, held, right_x)
    row_send(0, held, left_x)
    row_send(0, held, across)
    other = row_of(1 - zl, y, core)
    arrived(col_p.at[other], col_sem.at[other])
    col_send(other, right_y)
    col_send(other, left_y)
    col_send(other, sibling)

    before_x, after_x = (x + 3) % 4, (x + 1) % 4
    before_y, after_y = (y + 3) % 4, (y + 1) % 4
    row_arrived(0, across_held)
    row_send(0, across_held, right_x)
    row_send(0, across_held, left_x)

    def row_relay(u, h):
        for where, half, there in ((before_x, 0, right_x), (after_x, 1, left_x)):
            row_arrived(u, slot_at(where, h))
            row_send(u, slot_at(where, h), there, half)

    def col_relay(a):
        for where, half, there in ((before_y, 0, right_y), (after_y, 1, left_y)):
            index = row_of(a, where, core)
            arrived(col_p.at[index], col_sem.at[index])
            col_send(index, there, half)
            col_send(index, sibling)

    for k in range(2, 6):
        turn(k)
    row_relay(0, zh)
    col_relay(zl)
    turn(6)
    turn(7)
    inputs[2].wait()
    inputs[3].wait()
    pltpu.make_async_copy(sizes.at[pl.ds(0, 15)], sizes.at[pl.ds(0, 15)], size_sem).wait()
    pltpu.make_async_copy(sizes.at[pl.ds(0, 15)], sizes.at[pl.ds(0, 15)], size_send).wait()

    def sizes_of(index):
        return sizes[index, 0:1, :].astype(F32)

    order, last = plan(
        sizes_of(row), sizes_of(2 * col), sizes_of(2 * col + 1),
        [(cols_v[s:s + 1, :] & 255).astype(F32) for s in range(4)],
    )
    for k in range(4):
        meta_v[k:k + 1, :] = order[k].astype(I32)
    for k in range(8):
        meta_v[4 + k:5 + k, :] = last[k].astype(I32)
    to_scalars = pltpu.make_async_copy(meta_v, meta_s, meta_sem)
    to_scalars.start()

    row_relay(0, 1 - zh)
    col_relay(1 - zl)
    first_step(1)
    pick(0)
    pick(1)
    for a in (zl, 1 - zl):
        index = row_of(a, (y + 2) % 4, core)
        arrived(col_p.at[index], col_sem.at[index])
        col_send(index, sibling)
    pick(2)
    pick(3)
    to_scalars.wait()
    own.wait()
    for slot in (held, across_held, *[slot_at(w, h) for w in (before_x, after_x) for h in (0, 1)]):
        flip(0, slot)
    for k in range(4, 8):
        pick(k)
    for h in (zh, 1 - zh):
        slot = slot_at((x + 2) % 4, h)
        row_arrived(0, slot)
        flip(0, slot)
    for a in (zl, 1 - zl):
        for d in (0, 1, 3, 2):
            index = row_of(a, (y + d) % 4, 1 - core)
            arrived(col_p.at[index], col_sem.at[index])

    seq[TILES] = jnp.zeros((32, 128), F32)
    running[...] = jnp.zeros((32, 128), F32)

    def exchange_copy(there, u, ranks):
        return pltpu.make_async_remote_copy(
            src_ref=parts.at[there[0], u, ranks],
            dst_ref=got.at[row, u, ranks],
            send_sem=part_send.at[there[0]],
            recv_sem=part_sem.at[row],
            device_id=there,
            device_id_type=MESH,
        )

    def chunks(u, begin, end, width=2):
        @pl.loop(begin, end)
        def _(q):
            @pl.loop(0, 32 * width // GROUP)
            def _(m):
                start = 32 * width * q + GROUP * m
                before = jnp.maximum(start - 1, 0)
                previous = jnp.where(start == 0, -1, meta_s[before >> 7, before & 127] >> 9)
                rows, keeps, rights = [], [], []
                for g in range(GROUP):
                    n = start + g
                    code = meta_s[n >> 7, n & 127]
                    key = code >> 9
                    keeps.append(key == previous)
                    previous = key
                    i = code & 127
                    rows.append(i)
                    if u == 0:
                        j = cols_s[(code >> 7) & 3, i] & 255
                        rights.append(
                            jnp.dot(
                                a_buf[code & 511], col_p[j >> 4, (j >> 1) & 7],
                                preferred_element_type=F32,
                            ).astype(BF)
                        )
                        products[n] = rights[g]
                    else:
                        rights.append(products[n])
                pieces = [
                    jnp.dot(left[u, rows[g]], rights[g], preferred_element_type=F32)
                    for g in range(GROUP)
                ]
                total = running[...]
                for g in range(GROUP):
                    total = pieces[g] + jnp.where(keeps[g], total, 0.0)
                    seq[start + g] = total
                running[...] = total

            @pl.loop(0, ROWS, unroll=4)
            def _(d):
                for h in range(width):
                    key = 64 * (width * q + h) + 4 * d
                    even, even_far, odd_far, odd = [
                        seq[jnp.clip(meta_s[4 + (key >> 7), (key & 127) + c], 0, TILES)]
                        for c in range(4)
                    ]
                    near = jnp.where(lane[:32] == 0, even, odd)
                    far = jnp.where(lane[:32] == 0, odd_far, even_far)
                    parts[d, u, width * q + h] = (near + pltpu.roll(far, 64, 1)).astype(BF)

            for there in peers:
                exchange_copy(there, u, pl.ds(width * q, width)).start()

    chunks(0, 0, 2, 1)
    row_arrived(1, held)
    row_send(1, held, right_x)
    row_send(1, held, left_x)
    row_send(1, held, across)
    chunks(0, 1, 3)
    @pl.loop(0, ROWS)
    def _(k):
        ranks_v[pl.ds(k, 1), :] = ranks_of(sizes_of(k)).astype(I32)

    ranks_copy = pltpu.make_async_copy(ranks_v, ranks_out, local_sem)
    ranks_copy.start()
    row_arrived(1, across_held)
    row_send(1, across_held, right_x)
    row_send(1, across_held, left_x)
    row_relay(1, zh)
    chunks(0, 3, 5)
    row_relay(1, 1 - zh)
    chunks(0, 5, 8)
    for h in (zh, 1 - zh):
        row_arrived(1, slot_at((x + 2) % 4, h))
    for slot in range(8):
        flip(1, slot)
    chunks(1, 0, 8)

    mine_copy = pltpu.make_async_copy(parts.at[row], got.at[row], part_send.at[row])
    mine_copy.start()

    @pl.when(moves)
    def _():
        first(0).wait_send()
        first(1).wait_send()

    for copy in sent:
        copy.wait_send()
    ranks_copy.wait()
    mine_copy.wait()
    for there in peers:
        arrived(parts.at[there[0]], part_send.at[there[0]])
        arrived(got.at[there[0]], part_sem.at[there[0]])


def fused(p_tiles, sizes, a_cols, a_turned):
    hbm = pl.BlockSpec(memory_space=pltpu.HBM)
    free = pl.BlockSpec(memory_space=pl.ANY)
    dma = pltpu.SemaphoreType.DMA
    return pl.pallas_call(
        fused_kernel,
        out_shape=(
            jax.ShapeDtypeStruct((ROWS, 2, 16, 32, 128), BF),
            jax.ShapeDtypeStruct((ROWS, 128), I32),
        ),
        in_specs=[hbm] * 4,
        out_specs=[free, free],
        scratch_shapes=[
            pltpu.VMEM((16, 64, 64), BF),
            pltpu.VMEM((1, 16), I32),
            pltpu.VMEM((4, 128), I32),
            pltpu.SMEM((4, 128), I32),
            pltpu.VMEM((ROWS, 8, 128), I32),
            pltpu.VMEM((8, 64, 128), BF),
            pltpu.VMEM((2, 256, 128), BF),
            pltpu.VMEM((ROWS, 8, 64, 128), BF),
            pltpu.VMEM((2, 8, 256, 128), BF),
            pltpu.VMEM((4, 64, 64, 128), BF),
            pltpu.VMEM((128 * PITCH, 128), F32),
            pltpu.VMEM((TILES, 64, 64), BF),
            pltpu.VMEM((2, 128, 32, 64), BF),
            pltpu.VMEM((TILES, 64, 128), BF),
            pltpu.VMEM((TILES + 1, 32, 128), F32),
            pltpu.VMEM((32, 128), F32),
            pltpu.VMEM((ROWS, 2, 16, 32, 128), BF),
            pltpu.VMEM((16, 128), I32),
            pltpu.SMEM((16, 128), I32),
            pltpu.VMEM((ROWS, 128), I32),
            dma((4,)),
            dma((35,)),
            dma((ROWS,)),
            dma((2, 8)),
            dma((2,)),
            dma,
            dma,
            dma,
            dma((8,)),
            dma,
            dma((ROWS,)),
            dma((ROWS,)),
        ],
        compiler_params=pltpu.CompilerParams(
            collective_id=0, has_side_effects=True, vmem_limit_bytes=58 * MIB
        ),
    )(p_tiles, sizes, a_cols, a_turned)


def widen_kernel(ranks_hbm, got, out_hbm, ranks, narrow, wide, ranks_sem, in_sem, sem):
    def fetch(k):
        return pltpu.make_async_copy(got.at[k], narrow.at[k], in_sem.at[k])

    def copy(k):
        return pltpu.make_async_copy(wide.at[k % 8], out_hbm.at[pl.ds(16 * k, 16)], sem.at[k % 8])

    ranks_copy = pltpu.make_async_copy(ranks_hbm, ranks, ranks_sem)
    ranks_copy.start()
    for k in range(ROWS):
        fetch(k).start()
    ranks_copy.wait()
    for k in range(ROWS):
        if k >= 8:
            copy(k - 8).wait()
        fetch(k).wait()

        @pl.loop(0, 16, unroll=4)
        def _(a):
            for h in range(2):
                wide[k % 8, a, 32 * h:32 * h + 32] = narrow[k, h, ranks[k, a]].astype(F32)

        copy(k).start()
    for k in range(ROWS - 8, ROWS):
        copy(k).wait()


def widen(ranks, got):
    free = pl.BlockSpec(memory_space=pl.ANY)
    return pl.pallas_call(
        widen_kernel,
        out_shape=jax.ShapeDtypeStruct((256, 64, 128), F32),
        in_specs=[free, free],
        out_specs=free,
        scratch_shapes=[
            pltpu.SMEM((ROWS, 128), I32),
            pltpu.VMEM((ROWS, 2, 16, 32, 128), BF),
            pltpu.VMEM((8, 16, 64, 128), F32),
            pltpu.SemaphoreType.DMA,
            pltpu.SemaphoreType.DMA((ROWS,)),
            pltpu.SemaphoreType.DMA((8,)),
        ],
        compiler_params=pltpu.CompilerParams(vmem_limit_bytes=58 * MIB),
    )(ranks, got)


def per_device(a_tiles, a_cols, p_tiles, agg_sizes):
    got, ranks = fused(p_tiles, agg_sizes, a_cols.T, a_tiles.transpose(1, 2, 3, 0))
    return widen(ranks, got)


def solution(mesh):
    return jax.shard_map(
        per_device,
        mesh=mesh,
        in_specs=(
            P("row", "col", None, None),
            P("row", "col"),
            P(("col", "row"), None, None),
            P("row", None),
        ),
        out_specs=P(None, None, ("col", "row")),
        check_vma=False,
    )
```

```python
import jax
import jax.numpy as jnp
from jax import lax
from jax.experimental import pallas as pl
from jax.experimental.pallas import tpu as pltpu
from jax.sharding import PartitionSpec as P

MESH = pl.DeviceIdType.MESH
ROWS = 16
COLS = 8
MIB = 1 << 20
PITCH = 136
TILES = 512
GROUP = 32
BF = jnp.bfloat16
F32 = jnp.float32
I32 = jnp.int32

ORDER = [
    (0, 1, 0), (0, 3, 0), (1, 0, 0), (1, 2, 0), (0, 2, 0), (1, 1, 0), (1, 3, 0),
    (0, 1, 1), (0, 3, 1), (1, 0, 1), (1, 2, 1), (0, 2, 1), (1, 1, 1), (1, 3, 1), (0, 0, 1),
]


def place(zl, y, core, zh, x):
    return (zl * 8 + y * 2 + core, zh * 4 + x)


def iota(shape, dim):
    return lax.broadcasted_iota(I32, shape, dim).astype(F32)


def to_column(row):
    eye = iota((128, 128), 0) == iota((128, 128), 1)
    return jnp.sum(jnp.where(eye, row, 0.0), axis=1, keepdims=True)


def ranks_of(sizes):
    column = to_column(sizes)[:16]
    ahead = jnp.logical_or(
        column < sizes,
        jnp.logical_and(column == sizes, iota((16, 128), 0) < iota((16, 128), 1)),
    )
    return jnp.sum(jnp.where(ahead, 1.0, 0.0), axis=0, keepdims=True)


def ends_column(sizes):
    upto = iota((16, 128), 1) <= iota((16, 128), 0)
    return jnp.sum(jnp.where(upto, sizes, 0.0), axis=1, keepdims=True)


def aggregates(sizes):
    ends = ends_column(sizes)
    return jnp.sum(jnp.where(ends <= iota((16, 128), 1), 1.0, 0.0), axis=0, keepdims=True)


def plan(own_sizes, low_sizes, high_sizes, local_cols):
    owner = aggregates(own_sizes)
    rank_column = to_column(ranks_of(own_sizes))[:16]
    row_rank = jnp.sum(
        jnp.where(iota((16, 128), 0) == owner, rank_column, 0.0), axis=0, keepdims=True
    )
    low_column = to_column(aggregates(low_sizes))
    high_column = to_column(aggregates(high_sizes) + 16.0)
    codes = []
    for s in range(4):
        j = local_cols[s]
        target = jnp.sum(
            jnp.where(iota((128, 128), 0) == j, low_column, 0.0)
            + jnp.where(iota((128, 128), 0) + 128.0 == j, high_column, 0.0),
            axis=0, keepdims=True,
        )
        key = row_rank * 64.0 + target * 2.0 + (j - 2.0 * jnp.floor(j * 0.5))
        codes.append(key * 512.0 + (iota((1, 128), 1) + 128.0 * s))
    columns = [to_column(code) for code in codes]
    places = []
    for s in range(4):
        places.append(sum(
            jnp.sum(jnp.where(column < codes[s], 1.0, 0.0), axis=0, keepdims=True)
            for column in columns
        ))
    place_columns = [to_column(p) for p in places]
    order, last = [], []
    for s in range(4):
        n = iota((128, 128), 1) + 128.0 * s
        order.append(sum(
            jnp.sum(jnp.where(place_columns[q] == n, columns[q], 0.0), axis=0, keepdims=True)
            for q in range(4)
        ))
    key_columns = [jnp.floor(column * (1.0 / 512.0)) for column in columns]
    for s in range(8):
        n = iota((128, 128), 1) + 128.0 * s
        at = [
            jnp.max(jnp.where(key_columns[q] == n, place_columns[q], -1.0), axis=0, keepdims=True)
            for q in range(4)
        ]
        at = jnp.maximum(jnp.maximum(at[0], at[1]), jnp.maximum(at[2], at[3]))
        last.append(jnp.where(at < 0.0, float(TILES), at))
    return order, last


def fused_kernel(p_hbm, s_hbm, cols_hbm, a_hbm, got, ranks_out,
                 p_in, s_in, cols_v, cols_s, sizes, mine, mine_left, col_p, row_p, a_in, mid, a_buf,
                 left, products, seq, running, parts, meta_v, meta_s, ranks_v,
                 in_sem, send_sem, col_sem, row_sem, first_sem, size_send, size_sem, local_sem, a_sem,
                 meta_sem, part_send, part_sem):
    row = lax.axis_index("row")
    col = lax.axis_index("col")
    zl, y, core = row // 8, (row // 2) % 4, row % 2
    zh, x = col // 4, col % 4

    sibling = place(zl, y, 1 - core, zh, x)
    partner = place(1 - zl, y, core, zh, x)
    along_y = [place(zl, (y + d) % 4, core, zh, x) for d in (1, 3)]
    across = place(zl, y, core, 1 - zh, x)
    along_x = [place(zl, y, core, zh, (x + d) % 4) for d in (1, 3)]
    peers = [place((zl + a) % 2, (y + b) % 4, (core + c) % 2, zh, x) for a, b, c in ORDER]
    to = place(zh, x, zl, core, (x + y) % 4)
    source = place(core, (x - y + 4) % 4, zh, zl, y)
    stays = jnp.logical_and(to[0] == row, to[1] == col)
    moves = jnp.logical_not(stays)

    inputs = [
        pltpu.make_async_copy(s_hbm, s_in, in_sem.at[0]),
        pltpu.make_async_copy(p_hbm, p_in, in_sem.at[1]),
        pltpu.make_async_copy(cols_hbm, cols_v, in_sem.at[2]),
        pltpu.make_async_copy(cols_hbm, cols_s, in_sem.at[3]),
    ]
    for copy in inputs:
        copy.start()

    def a_copy(k):
        return pltpu.make_async_copy(
            a_hbm.at[:, pl.ds(8 * k, 8)], a_in.at[:, pl.ds(8 * k, 8)], a_sem.at[k]
        )

    for k in range(8):
        a_copy(k).start()

    barrier = pltpu.get_barrier_semaphore()
    for there in [*peers, across, *along_x]:
        pl.semaphore_signal(barrier, 1, device_id=there, device_id_type=MESH)

    @pl.when(moves)
    def _():
        pl.semaphore_signal(barrier, 1, device_id=source, device_id_type=MESH)

    inputs[0].wait()
    s_row = jnp.zeros((8, 128), I32)
    sizes[pl.ds(row, 1)] = s_row[None]
    sizes[row, 0:1, 0:16] = s_in[...]
    inputs[1].wait()
    for k in range(8):
        mine[k] = jnp.concatenate([p_in[2 * k], p_in[2 * k + 1]], axis=-1)
    for h in range(2):
        for k in range(4):
            mine_left[h, pl.ds(64 * k, 64), :] = jnp.concatenate(
                [p_in[4 * k + n][:, 32 * h:32 * h + 32] for n in range(4)], axis=-1
            )

    pl.semaphore_wait(barrier, 18 + jnp.where(stays, 0, 1))

    count = [0]
    sent = []

    def send(src, dst, sem, there):
        k = count[0]
        count[0] += 1
        copy = pltpu.make_async_remote_copy(
            src_ref=src, dst_ref=dst, send_sem=send_sem.at[k], recv_sem=sem,
            device_id=there, device_id_type=MESH,
        )
        copy.start()
        sent.append(copy)

    def arrived(ref, sem):
        pltpu.make_async_copy(ref, ref, sem).wait()

    def row_of(a, b, c):
        return a * 8 + b * 2 + c

    def slot_at(x, h):
        return 2 * ((x - y + 4) % 4) + h

    held, across_held = slot_at(x, zh), slot_at(x, 1 - zh)

    def first(u):
        return pltpu.make_async_remote_copy(
            src_ref=mine_left.at[u], dst_ref=row_p.at[u, 2 * y + core],
            send_sem=first_sem.at[u], recv_sem=row_sem.at[u, 2 * y + core],
            device_id=to, device_id_type=MESH,
        )

    def first_step(u):
        @pl.when(moves)
        def _():
            first(u).start()

        @pl.when(stays)
        def _():
            pltpu.make_async_copy(
                mine_left.at[u], row_p.at[u, 2 * y + core], row_sem.at[u, 2 * y + core]
            ).start()

    first_step(0)

    for there in peers:
        pltpu.make_async_remote_copy(
            src_ref=sizes.at[row], dst_ref=sizes.at[row], send_sem=size_send, recv_sem=size_sem,
            device_id=there, device_id_type=MESH,
        ).start()

    def col_send(index, there, half=None):
        pairs = pl.ds(0, 8) if half is None else pl.ds(4 * half, 4)
        ref = col_p.at[index, pairs]
        send(mine if index is row else ref, ref, col_sem.at[index], there)

    def row_send(u, slot, there, half=None):
        rows = pl.ds(0, 256) if half is None else pl.ds(128 * half, 128)
        ref = row_p.at[u, slot, rows]
        send(ref, ref, row_sem.at[u, slot], there)

    def row_arrived(u, slot):
        arrived(row_p.at[u, slot], row_sem.at[u, slot])

    right_y, left_y = along_y
    right_x, left_x = along_x
    for there in (partner, right_y, left_y, sibling):
        col_send(row, there)
    own = pltpu.make_async_copy(mine, col_p.at[row], local_sem)
    own.start()

    def turn(k):
        a_copy(k).wait()

        @pl.loop(0, 8, unroll=2)
        def _(n):
            u = 8 * k + n
            wide = jnp.concatenate([a_in[s, u] for s in range(4)], axis=0)
            tiles = wide.T.astype(F32)
            for h in range(2):
                at = pl.multiple_of(PITCH * (64 * h + u), 8)
                mid[pl.ds(at, 128), :] = tiles[:, 128 * h:128 * h + 128]

    def pick(k):
        @pl.loop(0, 16, unroll=4)
        def _(n):
            i = 16 * k + n
            for h in range(2):
                both = mid[pl.ds(64 * PITCH * h + i, 64, stride=PITCH), :]
                a_buf[256 * h + i] = both[:, :64].astype(BF)
                a_buf[256 * h + 128 + i] = pltpu.roll(both, 64, 1)[:, :64].astype(BF)

    lane = lax.broadcasted_iota(I32, (64, 128), 1) // 64

    def flip(u, slot):
        for k in range(4):
            turned = row_p[u, slot, 64 * k:64 * k + 64, :].T
            for n in range(4):
                left[u, 16 * slot + 4 * k + n] = turned[32 * n:32 * n + 32]

    for k in range(8):
        turn(k)

    row_arrived(0, held)
    row_send(0, held, right_x)
    row_send(0, held, left_x)
    row_send(0, held, across)
    other = row_of(1 - zl, y, core)
    arrived(col_p.at[other], col_sem.at[other])
    col_send(other, right_y)
    col_send(other, left_y)
    col_send(other, sibling)

    inputs[2].wait()
    inputs[3].wait()
    pltpu.make_async_copy(sizes.at[pl.ds(0, 15)], sizes.at[pl.ds(0, 15)], size_sem).wait()
    pltpu.make_async_copy(sizes.at[pl.ds(0, 15)], sizes.at[pl.ds(0, 15)], size_send).wait()

    def sizes_of(index):
        return sizes[index, 0:1, :].astype(F32)

    order, last = plan(
        sizes_of(row), sizes_of(2 * col), sizes_of(2 * col + 1),
        [(cols_v[s:s + 1, :] & 255).astype(F32) for s in range(4)],
    )
    for k in range(4):
        meta_v[k:k + 1, :] = order[k].astype(I32)
    for k in range(8):
        meta_v[4 + k:5 + k, :] = last[k].astype(I32)
    to_scalars = pltpu.make_async_copy(meta_v, meta_s, meta_sem)
    to_scalars.start()

    before_x, after_x = (x + 3) % 4, (x + 1) % 4
    before_y, after_y = (y + 3) % 4, (y + 1) % 4
    row_arrived(0, across_held)
    row_send(0, across_held, right_x)
    row_send(0, across_held, left_x)

    def row_relay(u, h):
        for where, half, there in ((before_x, 0, right_x), (after_x, 1, left_x)):
            row_arrived(u, slot_at(where, h))
            row_send(u, slot_at(where, h), there, half)

    def col_relay(a):
        for where, half, there in ((before_y, 0, right_y), (after_y, 1, left_y)):
            index = row_of(a, where, core)
            arrived(col_p.at[index], col_sem.at[index])
            col_send(index, there, half)
            col_send(index, sibling)

    row_relay(0, zh)
    col_relay(zl)
    pick(0)
    pick(1)
    row_relay(0, 1 - zh)
    col_relay(1 - zl)
    first_step(1)
    for a in (zl, 1 - zl):
        index = row_of(a, (y + 2) % 4, core)
        arrived(col_p.at[index], col_sem.at[index])
        col_send(index, sibling)
    pick(2)
    pick(3)
    to_scalars.wait()
    own.wait()
    for slot in (held, across_held, *[slot_at(w, h) for w in (before_x, after_x) for h in (0, 1)]):
        flip(0, slot)
    for k in range(4, 8):
        pick(k)
    for h in (zh, 1 - zh):
        slot = slot_at((x + 2) % 4, h)
        row_arrived(0, slot)
        flip(0, slot)
    for a in (zl, 1 - zl):
        for d in (0, 1, 3, 2):
            index = row_of(a, (y + d) % 4, 1 - core)
            arrived(col_p.at[index], col_sem.at[index])

    seq[TILES] = jnp.zeros((32, 128), F32)
    running[...] = jnp.zeros((32, 128), F32)

    def exchange_copy(there, u, ranks):
        return pltpu.make_async_remote_copy(
            src_ref=parts.at[there[0], u, ranks],
            dst_ref=got.at[row, u, ranks],
            send_sem=part_send.at[there[0]],
            recv_sem=part_sem.at[row],
            device_id=there,
            device_id_type=MESH,
        )

    def chunks(u, begin, end, width=2):
        @pl.loop(begin, end)
        def _(q):
            @pl.loop(0, 32 * width // GROUP)
            def _(m):
                start = 32 * width * q + GROUP * m
                before = jnp.maximum(start - 1, 0)
                previous = jnp.where(start == 0, -1, meta_s[before >> 7, before & 127] >> 9)
                rows, keeps, rights = [], [], []
                for g in range(GROUP):
                    n = start + g
                    code = meta_s[n >> 7, n & 127]
                    key = code >> 9
                    keeps.append(key == previous)
                    previous = key
                    i = code & 127
                    rows.append(i)
                    if u == 0:
                        j = cols_s[(code >> 7) & 3, i] & 255
                        rights.append(
                            jnp.dot(
                                a_buf[code & 511], col_p[j >> 4, (j >> 1) & 7],
                                preferred_element_type=F32,
                            ).astype(BF)
                        )
                        products[n] = rights[g]
                    else:
                        rights.append(products[n])
                pieces = [
                    jnp.dot(left[u, rows[g]], rights[g], preferred_element_type=F32)
                    for g in range(GROUP)
                ]
                total = running[...]
                for g in range(GROUP):
                    total = pieces[g] + jnp.where(keeps[g], total, 0.0)
                    seq[start + g] = total
                running[...] = total

            @pl.loop(0, ROWS, unroll=4)
            def _(d):
                for h in range(width):
                    key = 64 * (width * q + h) + 4 * d
                    even, even_far, odd_far, odd = [
                        seq[jnp.clip(meta_s[4 + (key >> 7), (key & 127) + c], 0, TILES)]
                        for c in range(4)
                    ]
                    near = jnp.where(lane[:32] == 0, even, odd)
                    far = jnp.where(lane[:32] == 0, odd_far, even_far)
                    parts[d, u, width * q + h] = (near + pltpu.roll(far, 64, 1)).astype(BF)

            for there in peers:
                exchange_copy(there, u, pl.ds(width * q, width)).start()

    chunks(0, 0, 2, 1)
    row_arrived(1, held)
    row_send(1, held, right_x)
    row_send(1, held, left_x)
    row_send(1, held, across)
    chunks(0, 1, 3)
    @pl.loop(0, ROWS)
    def _(k):
        ranks_v[pl.ds(k, 1), :] = ranks_of(sizes_of(k)).astype(I32)

    ranks_copy = pltpu.make_async_copy(ranks_v, ranks_out, local_sem)
    ranks_copy.start()
    row_arrived(1, across_held)
    row_send(1, across_held, right_x)
    row_send(1, across_held, left_x)
    row_relay(1, zh)
    chunks(0, 3, 5)
    row_relay(1, 1 - zh)
    chunks(0, 5, 8)
    for h in (zh, 1 - zh):
        row_arrived(1, slot_at((x + 2) % 4, h))
    for slot in range(8):
        flip(1, slot)
    chunks(1, 0, 8)

    mine_copy = pltpu.make_async_copy(parts.at[row], got.at[row], part_send.at[row])
    mine_copy.start()

    @pl.when(moves)
    def _():
        first(0).wait_send()
        first(1).wait_send()

    for copy in sent:
        copy.wait_send()
    ranks_copy.wait()
    mine_copy.wait()
    for there in peers:
        arrived(parts.at[there[0]], part_send.at[there[0]])
        arrived(got.at[there[0]], part_sem.at[there[0]])


def fused(p_tiles, sizes, a_cols, a_turned):
    hbm = pl.BlockSpec(memory_space=pltpu.HBM)
    free = pl.BlockSpec(memory_space=pl.ANY)
    dma = pltpu.SemaphoreType.DMA
    return pl.pallas_call(
        fused_kernel,
        out_shape=(
            jax.ShapeDtypeStruct((ROWS, 2, 16, 32, 128), BF),
            jax.ShapeDtypeStruct((ROWS, 128), I32),
        ),
        in_specs=[hbm] * 4,
        out_specs=[free, free],
        scratch_shapes=[
            pltpu.VMEM((16, 64, 64), BF),
            pltpu.VMEM((1, 16), I32),
            pltpu.VMEM((4, 128), I32),
            pltpu.SMEM((4, 128), I32),
            pltpu.VMEM((ROWS, 8, 128), I32),
            pltpu.VMEM((8, 64, 128), BF),
            pltpu.VMEM((2, 256, 128), BF),
            pltpu.VMEM((ROWS, 8, 64, 128), BF),
            pltpu.VMEM((2, 8, 256, 128), BF),
            pltpu.VMEM((4, 64, 64, 128), BF),
            pltpu.VMEM((128 * PITCH, 128), F32),
            pltpu.VMEM((TILES, 64, 64), BF),
            pltpu.VMEM((2, 128, 32, 64), BF),
            pltpu.VMEM((TILES, 64, 128), BF),
            pltpu.VMEM((TILES + 1, 32, 128), F32),
            pltpu.VMEM((32, 128), F32),
            pltpu.VMEM((ROWS, 2, 16, 32, 128), BF),
            pltpu.VMEM((16, 128), I32),
            pltpu.SMEM((16, 128), I32),
            pltpu.VMEM((ROWS, 128), I32),
            dma((4,)),
            dma((35,)),
            dma((ROWS,)),
            dma((2, 8)),
            dma((2,)),
            dma,
            dma,
            dma,
            dma((8,)),
            dma,
            dma((ROWS,)),
            dma((ROWS,)),
        ],
        compiler_params=pltpu.CompilerParams(
            collective_id=0, has_side_effects=True, vmem_limit_bytes=58 * MIB
        ),
    )(p_tiles, sizes, a_cols, a_turned)


def widen_kernel(ranks_hbm, got, out_hbm, ranks, narrow, wide, ranks_sem, in_sem, sem):
    def fetch(k):
        return pltpu.make_async_copy(got.at[k], narrow.at[k], in_sem.at[k])

    def copy(k):
        return pltpu.make_async_copy(wide.at[k % 8], out_hbm.at[pl.ds(16 * k, 16)], sem.at[k % 8])

    ranks_copy = pltpu.make_async_copy(ranks_hbm, ranks, ranks_sem)
    ranks_copy.start()
    for k in range(ROWS):
        fetch(k).start()
    ranks_copy.wait()
    for k in range(ROWS):
        if k >= 8:
            copy(k - 8).wait()
        fetch(k).wait()

        @pl.loop(0, 16, unroll=4)
        def _(a):
            for h in range(2):
                wide[k % 8, a, 32 * h:32 * h + 32] = narrow[k, h, ranks[k, a]].astype(F32)

        copy(k).start()
    for k in range(ROWS - 8, ROWS):
        copy(k).wait()


def widen(ranks, got):
    free = pl.BlockSpec(memory_space=pl.ANY)
    return pl.pallas_call(
        widen_kernel,
        out_shape=jax.ShapeDtypeStruct((256, 64, 128), F32),
        in_specs=[free, free],
        out_specs=free,
        scratch_shapes=[
            pltpu.SMEM((ROWS, 128), I32),
            pltpu.VMEM((ROWS, 2, 16, 32, 128), BF),
            pltpu.VMEM((8, 16, 64, 128), F32),
            pltpu.SemaphoreType.DMA,
            pltpu.SemaphoreType.DMA((ROWS,)),
            pltpu.SemaphoreType.DMA((8,)),
        ],
        compiler_params=pltpu.CompilerParams(vmem_limit_bytes=58 * MIB),
    )(ranks, got)


def per_device(a_tiles, a_cols, p_tiles, agg_sizes):
    got, ranks = fused(p_tiles, agg_sizes, a_cols.T, a_tiles.transpose(1, 2, 3, 0))
    return widen(ranks, got)


def solution(mesh):
    return jax.shard_map(
        per_device,
        mesh=mesh,
        in_specs=(
            P("row", "col", None, None),
            P("row", "col"),
            P(("col", "row"), None, None),
            P("row", None),
        ),
        out_specs=P(None, None, ("col", "row")),
        check_vma=False,
    )
```

```python
import jax
import jax.numpy as jnp
from jax import lax
from jax.experimental import pallas as pl
from jax.experimental.pallas import tpu as pltpu
from jax.sharding import PartitionSpec as P

MESH = pl.DeviceIdType.MESH
ROWS = 16
COLS = 8
MIB = 1 << 20
PITCH = 136
TILES = 512
GROUP = 32
BF = jnp.bfloat16
F32 = jnp.float32
I32 = jnp.int32

ORDER = [
    (0, 1, 0), (0, 3, 0), (1, 0, 0), (1, 2, 0), (0, 2, 0), (1, 1, 0), (1, 3, 0),
    (0, 1, 1), (0, 3, 1), (1, 0, 1), (1, 2, 1), (0, 2, 1), (1, 1, 1), (1, 3, 1), (0, 0, 1),
]


def place(zl, y, core, zh, x):
    return (zl * 8 + y * 2 + core, zh * 4 + x)


def iota(shape, dim):
    return lax.broadcasted_iota(I32, shape, dim).astype(F32)


def to_column(row):
    eye = iota((128, 128), 0) == iota((128, 128), 1)
    return jnp.sum(jnp.where(eye, row, 0.0), axis=1, keepdims=True)


def ranks_of(sizes):
    column = to_column(sizes)[:16]
    ahead = jnp.logical_or(
        column < sizes,
        jnp.logical_and(column == sizes, iota((16, 128), 0) < iota((16, 128), 1)),
    )
    return jnp.sum(jnp.where(ahead, 1.0, 0.0), axis=0, keepdims=True)


def ends_column(sizes):
    upto = iota((16, 128), 1) <= iota((16, 128), 0)
    return jnp.sum(jnp.where(upto, sizes, 0.0), axis=1, keepdims=True)


def aggregates(sizes):
    ends = ends_column(sizes)
    return jnp.sum(jnp.where(ends <= iota((16, 128), 1), 1.0, 0.0), axis=0, keepdims=True)


def plan(own_sizes, low_sizes, high_sizes, local_cols):
    owner = aggregates(own_sizes)
    rank_column = to_column(ranks_of(own_sizes))[:16]
    row_rank = jnp.sum(
        jnp.where(iota((16, 128), 0) == owner, rank_column, 0.0), axis=0, keepdims=True
    )
    low_column = to_column(aggregates(low_sizes))
    high_column = to_column(aggregates(high_sizes) + 16.0)
    codes = []
    for s in range(4):
        j = local_cols[s]
        target = jnp.sum(
            jnp.where(iota((128, 128), 0) == j, low_column, 0.0)
            + jnp.where(iota((128, 128), 0) + 128.0 == j, high_column, 0.0),
            axis=0, keepdims=True,
        )
        key = row_rank * 64.0 + target * 2.0 + (j - 2.0 * jnp.floor(j * 0.5))
        codes.append(key * 512.0 + (iota((1, 128), 1) + 128.0 * s))
    columns = [to_column(code) for code in codes]
    places = []
    for s in range(4):
        places.append(sum(
            jnp.sum(jnp.where(column < codes[s], 1.0, 0.0), axis=0, keepdims=True)
            for column in columns
        ))
    place_columns = [to_column(p) for p in places]
    order, last = [], []
    for s in range(4):
        n = iota((128, 128), 1) + 128.0 * s
        order.append(sum(
            jnp.sum(jnp.where(place_columns[q] == n, columns[q], 0.0), axis=0, keepdims=True)
            for q in range(4)
        ))
    key_columns = [jnp.floor(column * (1.0 / 512.0)) for column in columns]
    for s in range(8):
        n = iota((128, 128), 1) + 128.0 * s
        at = [
            jnp.max(jnp.where(key_columns[q] == n, place_columns[q], -1.0), axis=0, keepdims=True)
            for q in range(4)
        ]
        at = jnp.maximum(jnp.maximum(at[0], at[1]), jnp.maximum(at[2], at[3]))
        last.append(jnp.where(at < 0.0, float(TILES), at))
    return order, last


def fused_kernel(p_hbm, s_hbm, cols_hbm, a_hbm, got, ranks_out,
                 p_in, s_in, cols_v, cols_s, sizes, mine, mine_left, col_p, row_p, a_in, mid, a_buf,
                 left, products, seq, running, parts, meta_v, meta_s, ranks_v,
                 in_sem, send_sem, col_sem, row_sem, first_sem, size_send, size_sem, local_sem, a_sem,
                 meta_sem, part_send, part_sem):
    row = lax.axis_index("row")
    col = lax.axis_index("col")
    zl, y, core = row // 8, (row // 2) % 4, row % 2
    zh, x = col // 4, col % 4

    sibling = place(zl, y, 1 - core, zh, x)
    partner = place(1 - zl, y, core, zh, x)
    along_y = [place(zl, (y + d) % 4, core, zh, x) for d in (1, 3)]
    across = place(zl, y, core, 1 - zh, x)
    along_x = [place(zl, y, core, zh, (x + d) % 4) for d in (1, 3)]
    peers = [place((zl + a) % 2, (y + b) % 4, (core + c) % 2, zh, x) for a, b, c in ORDER]
    to = place(zh, x, zl, core, (x + y) % 4)
    source = place(core, (x - y + 4) % 4, zh, zl, y)
    stays = jnp.logical_and(to[0] == row, to[1] == col)
    moves = jnp.logical_not(stays)

    inputs = [
        pltpu.make_async_copy(s_hbm, s_in, in_sem.at[0]),
        pltpu.make_async_copy(p_hbm, p_in, in_sem.at[1]),
        pltpu.make_async_copy(cols_hbm, cols_v, in_sem.at[2]),
        pltpu.make_async_copy(cols_hbm, cols_s, in_sem.at[3]),
    ]
    for copy in inputs:
        copy.start()

    def a_copy(k):
        return pltpu.make_async_copy(
            a_hbm.at[:, pl.ds(8 * k, 8)], a_in.at[:, pl.ds(8 * k, 8)], a_sem.at[k]
        )

    for k in range(8):
        a_copy(k).start()

    barrier = pltpu.get_barrier_semaphore()
    for there in [*peers, across, *along_x]:
        pl.semaphore_signal(barrier, 1, device_id=there, device_id_type=MESH)

    @pl.when(moves)
    def _():
        pl.semaphore_signal(barrier, 1, device_id=source, device_id_type=MESH)

    inputs[0].wait()
    s_row = jnp.zeros((8, 128), I32)
    sizes[pl.ds(row, 1)] = s_row[None]
    sizes[row, 0:1, 0:16] = s_in[...]
    inputs[1].wait()
    for k in range(8):
        mine[k] = jnp.concatenate([p_in[2 * k], p_in[2 * k + 1]], axis=-1)
    for h in range(2):
        for k in range(4):
            mine_left[h, pl.ds(64 * k, 64), :] = jnp.concatenate(
                [p_in[4 * k + n][:, 32 * h:32 * h + 32] for n in range(4)], axis=-1
            )

    pl.semaphore_wait(barrier, 18 + jnp.where(stays, 0, 1))

    count = [0]
    sent = []

    def send(src, dst, sem, there):
        k = count[0]
        count[0] += 1
        copy = pltpu.make_async_remote_copy(
            src_ref=src, dst_ref=dst, send_sem=send_sem.at[k], recv_sem=sem,
            device_id=there, device_id_type=MESH,
        )
        copy.start()
        sent.append(copy)

    def arrived(ref, sem):
        pltpu.make_async_copy(ref, ref, sem).wait()

    def row_of(a, b, c):
        return a * 8 + b * 2 + c

    def slot_at(x, h):
        return 2 * ((x - y + 4) % 4) + h

    held, across_held = slot_at(x, zh), slot_at(x, 1 - zh)

    def first(u):
        return pltpu.make_async_remote_copy(
            src_ref=mine_left.at[u], dst_ref=row_p.at[u, 2 * y + core],
            send_sem=first_sem.at[u], recv_sem=row_sem.at[u, 2 * y + core],
            device_id=to, device_id_type=MESH,
        )

    def first_step(u):
        @pl.when(moves)
        def _():
            first(u).start()

        @pl.when(stays)
        def _():
            pltpu.make_async_copy(
                mine_left.at[u], row_p.at[u, 2 * y + core], row_sem.at[u, 2 * y + core]
            ).start()

    first_step(0)

    for there in peers:
        pltpu.make_async_remote_copy(
            src_ref=sizes.at[row], dst_ref=sizes.at[row], send_sem=size_send, recv_sem=size_sem,
            device_id=there, device_id_type=MESH,
        ).start()

    def col_send(index, there, half=None):
        pairs = pl.ds(0, 8) if half is None else pl.ds(4 * half, 4)
        ref = col_p.at[index, pairs]
        send(mine if index is row else ref, ref, col_sem.at[index], there)

    def row_send(u, slot, there, half=None):
        rows = pl.ds(0, 256) if half is None else pl.ds(128 * half, 128)
        ref = row_p.at[u, slot, rows]
        send(ref, ref, row_sem.at[u, slot], there)

    def row_arrived(u, slot):
        arrived(row_p.at[u, slot], row_sem.at[u, slot])

    right_y, left_y = along_y
    right_x, left_x = along_x
    for there in (partner, right_y, left_y, sibling):
        col_send(row, there)
    own = pltpu.make_async_copy(mine, col_p.at[row], local_sem)
    own.start()

    def turn(k):
        a_copy(k).wait()

        @pl.loop(0, 8, unroll=2)
        def _(n):
            u = 8 * k + n
            wide = jnp.concatenate([a_in[s, u] for s in range(4)], axis=0)
            tiles = wide.T.astype(F32)
            for h in range(2):
                at = pl.multiple_of(PITCH * (64 * h + u), 8)
                mid[pl.ds(at, 128), :] = tiles[:, 128 * h:128 * h + 128]

    def pick(k):
        @pl.loop(0, 16, unroll=4)
        def _(n):
            i = 16 * k + n
            for h in range(2):
                both = mid[pl.ds(64 * PITCH * h + i, 64, stride=PITCH), :]
                a_buf[256 * h + i] = both[:, :64].astype(BF)
                a_buf[256 * h + 128 + i] = pltpu.roll(both, 64, 1)[:, :64].astype(BF)

    lane = lax.broadcasted_iota(I32, (64, 128), 1) // 64

    def flip(u, slot):
        for k in range(4):
            turned = row_p[u, slot, 64 * k:64 * k + 64, :].T
            for n in range(4):
                left[u, 16 * slot + 4 * k + n] = turned[32 * n:32 * n + 32]

    for k in range(8):
        turn(k)

    row_arrived(0, held)
    row_send(0, held, right_x)
    row_send(0, held, left_x)
    row_send(0, held, across)
    other = row_of(1 - zl, y, core)
    arrived(col_p.at[other], col_sem.at[other])
    col_send(other, right_y)
    col_send(other, left_y)
    col_send(other, sibling)

    inputs[2].wait()
    inputs[3].wait()
    pltpu.make_async_copy(sizes.at[pl.ds(0, 15)], sizes.at[pl.ds(0, 15)], size_sem).wait()
    pltpu.make_async_copy(sizes.at[pl.ds(0, 15)], sizes.at[pl.ds(0, 15)], size_send).wait()

    def sizes_of(index):
        return sizes[index, 0:1, :].astype(F32)

    order, last = plan(
        sizes_of(row), sizes_of(2 * col), sizes_of(2 * col + 1),
        [(cols_v[s:s + 1, :] & 255).astype(F32) for s in range(4)],
    )
    for k in range(4):
        meta_v[k:k + 1, :] = order[k].astype(I32)
    for k in range(8):
        meta_v[4 + k:5 + k, :] = last[k].astype(I32)
    to_scalars = pltpu.make_async_copy(meta_v, meta_s, meta_sem)
    to_scalars.start()

    before_x, after_x = (x + 3) % 4, (x + 1) % 4
    before_y, after_y = (y + 3) % 4, (y + 1) % 4
    row_arrived(0, across_held)
    row_send(0, across_held, right_x)
    row_send(0, across_held, left_x)

    def row_relay(u, h):
        for where, half, there in ((before_x, 0, right_x), (after_x, 1, left_x)):
            row_arrived(u, slot_at(where, h))
            row_send(u, slot_at(where, h), there, half)

    def col_relay(a):
        for where, half, there in ((before_y, 0, right_y), (after_y, 1, left_y)):
            index = row_of(a, where, core)
            arrived(col_p.at[index], col_sem.at[index])
            col_send(index, there, half)
            col_send(index, sibling)

    row_relay(0, zh)
    col_relay(zl)
    pick(0)
    pick(1)
    row_relay(0, 1 - zh)
    col_relay(1 - zl)
    for a in (zl, 1 - zl):
        index = row_of(a, (y + 2) % 4, core)
        arrived(col_p.at[index], col_sem.at[index])
        col_send(index, sibling)
    first_step(1)
    pick(2)
    pick(3)
    to_scalars.wait()
    own.wait()
    for slot in (held, across_held, *[slot_at(w, h) for w in (before_x, after_x) for h in (0, 1)]):
        flip(0, slot)
    for k in range(4, 8):
        pick(k)
    for h in (zh, 1 - zh):
        slot = slot_at((x + 2) % 4, h)
        row_arrived(0, slot)
        flip(0, slot)
    for a in (zl, 1 - zl):
        for d in (0, 1, 3, 2):
            index = row_of(a, (y + d) % 4, 1 - core)
            arrived(col_p.at[index], col_sem.at[index])

    seq[TILES] = jnp.zeros((32, 128), F32)
    running[...] = jnp.zeros((32, 128), F32)

    def exchange_copy(there, u, ranks):
        return pltpu.make_async_remote_copy(
            src_ref=parts.at[there[0], u, ranks],
            dst_ref=got.at[row, u, ranks],
            send_sem=part_send.at[there[0]],
            recv_sem=part_sem.at[row],
            device_id=there,
            device_id_type=MESH,
        )

    def chunks(u, begin, end, width=2):
        @pl.loop(begin, end)
        def _(q):
            @pl.loop(0, 32 * width // GROUP)
            def _(m):
                start = 32 * width * q + GROUP * m
                before = jnp.maximum(start - 1, 0)
                previous = jnp.where(start == 0, -1, meta_s[before >> 7, before & 127] >> 9)
                rows, keeps, rights = [], [], []
                for g in range(GROUP):
                    n = start + g
                    code = meta_s[n >> 7, n & 127]
                    key = code >> 9
                    keeps.append(key == previous)
                    previous = key
                    i = code & 127
                    rows.append(i)
                    if u == 0:
                        j = cols_s[(code >> 7) & 3, i] & 255
                        rights.append(
                            jnp.dot(
                                a_buf[code & 511], col_p[j >> 4, (j >> 1) & 7],
                                preferred_element_type=F32,
                            ).astype(BF)
                        )
                        products[n] = rights[g]
                    else:
                        rights.append(products[n])
                pieces = [
                    jnp.dot(left[u, rows[g]], rights[g], preferred_element_type=F32)
                    for g in range(GROUP)
                ]
                total = running[...]
                for g in range(GROUP):
                    total = pieces[g] + jnp.where(keeps[g], total, 0.0)
                    seq[start + g] = total
                running[...] = total

            @pl.loop(0, ROWS, unroll=4)
            def _(d):
                for h in range(width):
                    key = 64 * (width * q + h) + 4 * d
                    even, even_far, odd_far, odd = [
                        seq[jnp.clip(meta_s[4 + (key >> 7), (key & 127) + c], 0, TILES)]
                        for c in range(4)
                    ]
                    near = jnp.where(lane[:32] == 0, even, odd)
                    far = jnp.where(lane[:32] == 0, odd_far, even_far)
                    parts[d, u, width * q + h] = (near + pltpu.roll(far, 64, 1)).astype(BF)

            for there in peers:
                exchange_copy(there, u, pl.ds(width * q, width)).start()

    chunks(0, 0, 2, 1)
    row_arrived(1, held)
    row_send(1, held, right_x)
    row_send(1, held, left_x)
    row_send(1, held, across)
    chunks(0, 1, 3)
    @pl.loop(0, ROWS)
    def _(k):
        ranks_v[pl.ds(k, 1), :] = ranks_of(sizes_of(k)).astype(I32)

    ranks_copy = pltpu.make_async_copy(ranks_v, ranks_out, local_sem)
    ranks_copy.start()
    row_arrived(1, across_held)
    row_send(1, across_held, right_x)
    row_send(1, across_held, left_x)
    row_relay(1, zh)
    chunks(0, 3, 5)
    row_relay(1, 1 - zh)
    chunks(0, 5, 8)
    for h in (zh, 1 - zh):
        row_arrived(1, slot_at((x + 2) % 4, h))
    for slot in range(8):
        flip(1, slot)
    chunks(1, 0, 8)

    mine_copy = pltpu.make_async_copy(parts.at[row], got.at[row], part_send.at[row])
    mine_copy.start()

    @pl.when(moves)
    def _():
        first(0).wait_send()
        first(1).wait_send()

    for copy in sent:
        copy.wait_send()
    ranks_copy.wait()
    mine_copy.wait()
    for there in peers:
        arrived(parts.at[there[0]], part_send.at[there[0]])
        arrived(got.at[there[0]], part_sem.at[there[0]])


def fused(p_tiles, sizes, a_cols, a_turned):
    hbm = pl.BlockSpec(memory_space=pltpu.HBM)
    free = pl.BlockSpec(memory_space=pl.ANY)
    dma = pltpu.SemaphoreType.DMA
    return pl.pallas_call(
        fused_kernel,
        out_shape=(
            jax.ShapeDtypeStruct((ROWS, 2, 16, 32, 128), BF),
            jax.ShapeDtypeStruct((ROWS, 128), I32),
        ),
        in_specs=[hbm] * 4,
        out_specs=[free, free],
        scratch_shapes=[
            pltpu.VMEM((16, 64, 64), BF),
            pltpu.VMEM((1, 16), I32),
            pltpu.VMEM((4, 128), I32),
            pltpu.SMEM((4, 128), I32),
            pltpu.VMEM((ROWS, 8, 128), I32),
            pltpu.VMEM((8, 64, 128), BF),
            pltpu.VMEM((2, 256, 128), BF),
            pltpu.VMEM((ROWS, 8, 64, 128), BF),
            pltpu.VMEM((2, 8, 256, 128), BF),
            pltpu.VMEM((4, 64, 64, 128), BF),
            pltpu.VMEM((128 * PITCH, 128), F32),
            pltpu.VMEM((TILES, 64, 64), BF),
            pltpu.VMEM((2, 128, 32, 64), BF),
            pltpu.VMEM((TILES, 64, 128), BF),
            pltpu.VMEM((TILES + 1, 32, 128), F32),
            pltpu.VMEM((32, 128), F32),
            pltpu.VMEM((ROWS, 2, 16, 32, 128), BF),
            pltpu.VMEM((16, 128), I32),
            pltpu.SMEM((16, 128), I32),
            pltpu.VMEM((ROWS, 128), I32),
            dma((4,)),
            dma((35,)),
            dma((ROWS,)),
            dma((2, 8)),
            dma((2,)),
            dma,
            dma,
            dma,
            dma((8,)),
            dma,
            dma((ROWS,)),
            dma((ROWS,)),
        ],
        compiler_params=pltpu.CompilerParams(
            collective_id=0, has_side_effects=True, vmem_limit_bytes=58 * MIB
        ),
    )(p_tiles, sizes, a_cols, a_turned)


def widen_kernel(ranks_hbm, got, out_hbm, ranks, narrow, wide, ranks_sem, in_sem, sem):
    def fetch(k):
        return pltpu.make_async_copy(got.at[k], narrow.at[k], in_sem.at[k])

    def copy(k):
        return pltpu.make_async_copy(wide.at[k % 8], out_hbm.at[pl.ds(16 * k, 16)], sem.at[k % 8])

    ranks_copy = pltpu.make_async_copy(ranks_hbm, ranks, ranks_sem)
    ranks_copy.start()
    for k in range(ROWS):
        fetch(k).start()
    ranks_copy.wait()
    for k in range(ROWS):
        if k >= 8:
            copy(k - 8).wait()
        fetch(k).wait()

        @pl.loop(0, 16, unroll=4)
        def _(a):
            for h in range(2):
                wide[k % 8, a, 32 * h:32 * h + 32] = narrow[k, h, ranks[k, a]].astype(F32)

        copy(k).start()
    for k in range(ROWS - 8, ROWS):
        copy(k).wait()


def widen(ranks, got):
    free = pl.BlockSpec(memory_space=pl.ANY)
    return pl.pallas_call(
        widen_kernel,
        out_shape=jax.ShapeDtypeStruct((256, 64, 128), F32),
        in_specs=[free, free],
        out_specs=free,
        scratch_shapes=[
            pltpu.SMEM((ROWS, 128), I32),
            pltpu.VMEM((ROWS, 2, 16, 32, 128), BF),
            pltpu.VMEM((8, 16, 64, 128), F32),
            pltpu.SemaphoreType.DMA,
            pltpu.SemaphoreType.DMA((ROWS,)),
            pltpu.SemaphoreType.DMA((8,)),
        ],
        compiler_params=pltpu.CompilerParams(vmem_limit_bytes=58 * MIB),
    )(ranks, got)


def per_device(a_tiles, a_cols, p_tiles, agg_sizes):
    got, ranks = fused(p_tiles, agg_sizes, a_cols.T, a_tiles.transpose(1, 2, 3, 0))
    return widen(ranks, got)


def solution(mesh):
    return jax.shard_map(
        per_device,
        mesh=mesh,
        in_specs=(
            P("row", "col", None, None),
            P("row", "col"),
            P(("col", "row"), None, None),
            P("row", None),
        ),
        out_specs=P(None, None, ("col", "row")),
        check_vma=False,
    )
```
